128 devices in a mesh: grp: 4 (over x), row: 32 (over y, z, core).
Axes of the slice: x: 4, y: 4, z: 4, core: 2. Of those that a mesh axis runs over, the one named last changes fastest.
Arguments:
- matrix_tiles: float32 [512, 32, 128, 128], P(('grp', 'row')), may hold values from -2 to 2, as said below
- column_index: int32 [512, 32], P(('grp', 'row')), may hold values from 0 to 511, as said below
- precond: float32 [512, 128, 128], P(('grp', 'row')), may hold values from -12 to 16, as said below
- right_side: float32 [512, 16, 128], P(('grp', 'row')), may hold values from -60 to 60
- lost_group: int32 [1], replicated, may hold values from 0 to 16383
Outputs:
- recovered: float32 [512, 16, 128], P(('grp', 'row'))
- true_residual: float32 [512, 16, 128], P(('grp', 'row'))
The draws below stay inside these ranges and needn't reach their ends.
Inputs may be any that keep to these rules, and one draw needn't show every extreme that they name: `column_index`: entry 0 of block row i is i; entry 1 is i + 12, or i - 12 where i + 12 passes the end; every entry lies within 12 of its block row. `precond`: every block is symmetric positive definite. `matrix_tiles`: the diagonal tile of each block row is near the identity.
All inputs are finite; a program needn't handle non-finite values.
Results may differ from the reference program's by a relative error of at most 0.0003.
Values sent between devices are 32-bit elements; how exact they have to be, the bound alone decides.
A program may use at most 64 MiB of HBM per device.

```python
import math
import jax
import jax.numpy as jnp
from jax import lax

TB = 128
K = 32
COLS = 16
BR = 4
OUTER = 2
INNER = 2
BAND = 12
NB = 512
N_GRP = 4
N_ROW = 32


def draw_matrix_tiles(key, part):
    shape_all = (NB, K, TB, TB)
    noise = jax.random.normal(key, shape_all, jnp.float32)
    off_scale = 0.2 / math.sqrt((K - 1) * TB)
    diag_scale = 0.15 / math.sqrt(TB)
    slots = jnp.arange(K, dtype=jnp.int32)[None, :, None, None]
    identity = jnp.eye(TB, dtype=jnp.float32)[None, None, :, :]
    return jnp.where(slots == 0, identity + diag_scale * noise, off_scale * noise)


def draw_column_index(key, part):
    key_reach, key_pick = jax.random.split(key)
    rows = jnp.arange(NB, dtype=jnp.int32)[:, None]
    reach = jax.random.randint(key_reach, (NB, 1), 1, BAND + 1, dtype=jnp.int32)
    picks = jax.random.randint(key_pick, (NB, K), 0, 1 << 20, dtype=jnp.int32)
    offsets = picks % (2 * reach + 1) - reach
    target = rows + offsets
    target = jnp.where((target < 0) | (target >= NB), rows - offsets, target)
    slots = jnp.arange(K, dtype=jnp.int32)[None, :]
    farthest = jnp.where(rows + BAND < NB, rows + BAND, rows - BAND)
    target = jnp.where(slots == 0, rows, jnp.where(slots == 1, farthest, target))
    return target.astype(jnp.int32)


def draw_precond(key, part):
    key_noise, key_scale = jax.random.split(key)
    noise = jax.random.normal(key_noise, (NB, TB, TB), jnp.float32)
    scales = jnp.exp(jax.random.uniform(key_scale, (NB, TB), jnp.float32, math.log(0.5), math.log(2.0)))
    symmetric = 0.5 * (noise + jnp.swapaxes(noise, 1, 2))
    core = jnp.eye(TB, dtype=jnp.float32)[None] + 0.3 / math.sqrt(TB) * symmetric
    return scales[:, :, None] * core * scales[:, None, :]


def draw_right_side(key, part):
    key_noise, key_cols = jax.random.split(key, 2)
    position = jnp.arange(NB, dtype=jnp.float32) / max(NB - 1, 1)
    col_scale = jnp.exp(jax.random.uniform(key_cols, (COLS,), jnp.float32, math.log(0.3), math.log(3.0)))
    noise = jax.random.normal(key_noise, (NB, COLS, TB), jnp.float32)
    rising = (1.0 + 2.0 * position) / 2.0
    return noise * rising[:, None, None] * col_scale[None, :, None]


def setup_inputs(seed: int = 0) -> dict:
    seeds = jax.random.split(jax.random.key(seed), 6)
    matrix_tiles = draw_matrix_tiles(jax.random.fold_in(seeds[5], 71), 0)
    column_index = draw_column_index(jax.random.fold_in(seeds[5], 71), 0)
    precond = draw_precond(jax.random.fold_in(seeds[5], 71), 0)
    right_side = draw_right_side(jax.random.fold_in(seeds[5], 71), 0)
    lost_group = jax.random.randint(seeds[4], (1,), 0, 4096 * N_GRP).astype(jnp.int32)
    return dict(matrix_tiles=matrix_tiles, column_index=column_index, precond=precond, right_side=right_side, lost_group=lost_group)


def inner_products(former, latter):
    return jnp.einsum('ica,ida->cd', former, latter, precision=lax.Precision.HIGHEST)

def scaled_by(vector, coeffs):
    return jnp.einsum('ica,cd->ida', vector, coeffs, precision=lax.Precision.HIGHEST)

def solve_sym(matrix, target):
    factor = jnp.linalg.cholesky(0.5 * (matrix + matrix.T))
    middle = lax.linalg.triangular_solve(factor, target, left_side=True, lower=True)
    return lax.linalg.triangular_solve(factor, middle, left_side=True, lower=True, transpose_a=True)

def products(matrix_tiles, column_index, vector, kept_mask):
    total = column_index.shape[0]
    tile_blocks = matrix_tiles.reshape(total // BR, BR, K, TB, TB)
    col_blocks = column_index.reshape(total // BR, BR, K)
    mask_blocks = kept_mask.reshape(total // BR, BR, K)

    def one_block(packed):
        tile_block, col_block, mask_block = packed
        picked = jnp.take(vector, col_block, axis=0) * mask_block[:, :, None, None]
        return jnp.einsum('ikab,ikcb->ica', tile_block, picked, precision=lax.Precision.HIGHEST)
    return lax.map(one_block, (tile_blocks, col_blocks, mask_blocks)).reshape(total, COLS, TB)

def reference(matrix_tiles, column_index, precond, right_side, lost_group):
    total = right_side.shape[0]
    group_blocks = BR * N_ROW
    all_ones = jnp.ones(column_index.shape, jnp.float32)
    row_group = (jnp.arange(total, dtype=jnp.int32) // group_blocks)[:, None]
    other_mask = (column_index // group_blocks != row_group).astype(jnp.float32)
    solution = jnp.zeros_like(right_side)
    residual = right_side
    direction = right_side
    squares = inner_products(residual, residual)
    for outer_step in range(OUTER):
        applied = products(matrix_tiles, column_index, direction, all_ones)
        advance = solve_sym(inner_products(direction, applied), squares)
        solution = solution + scaled_by(direction, advance)
        residual = residual - scaled_by(applied, advance)
        squares_next = inner_products(residual, residual)
        mixing = solve_sym(squares, squares_next)
        direction = residual + scaled_by(direction, mixing)
        squares = squares_next
    coupled = products(matrix_tiles, column_index, solution, other_mask)
    inner_target = right_side - coupled
    lost = (lost_group[0] % N_GRP).astype(jnp.int32)
    first_row = (lost * group_blocks).astype(jnp.int32)
    sub_tiles = lax.dynamic_slice_in_dim(matrix_tiles, first_row, group_blocks, 0)
    sub_cols = lax.dynamic_slice_in_dim(column_index, first_row, group_blocks, 0) - first_row
    sub_mask = ((sub_cols >= 0) & (sub_cols < group_blocks)).astype(jnp.float32)
    sub_cols = jnp.clip(sub_cols, 0, group_blocks - 1).astype(jnp.int32)
    sub_target = lax.dynamic_slice_in_dim(inner_target, first_row, group_blocks, 0)
    sub_inverse = lax.dynamic_slice_in_dim(precond, first_row, group_blocks, 0)

    def condition(vector):
        return jnp.einsum('iab,icb->ica', sub_inverse, vector, precision=lax.Precision.HIGHEST)
    estimate = jnp.zeros_like(sub_target)
    remainder = sub_target
    smoothed = condition(remainder)
    heading = smoothed
    weight = inner_products(remainder, smoothed)
    for inner_step in range(INNER):
        applied = products(sub_tiles, sub_cols, heading, sub_mask)
        advance = solve_sym(inner_products(heading, applied), weight)
        estimate = estimate + scaled_by(heading, advance)
        remainder = remainder - scaled_by(applied, advance)
        if inner_step + 1 < INNER:
            smoothed = condition(remainder)
            weight_next = inner_products(remainder, smoothed)
            heading = smoothed + scaled_by(heading, solve_sym(weight, weight_next))
            weight = weight_next
    recovered = lax.dynamic_update_slice_in_dim(solution, estimate, first_row, 0)
    true_residual = right_side - products(matrix_tiles, column_index, recovered, all_ones)
    return (recovered, true_residual)
```

```python
import functools

import jax
import jax.numpy as jnp
from jax import lax
from jax.experimental import pallas as pl
from jax.experimental.pallas import tpu as pltpu
from jax.sharding import PartitionSpec as P

BAND = 12
F32 = jnp.float32
BF16 = jnp.bfloat16
MESH = pl.DeviceIdType.MESH
N_GRP, N_ROW, BR, K, COLS, TB = 4, 32, 4, 32, 16, 128
REACH = 3
WIN = BR * (2 * REACH + 1)
CELL = 8
FAR = (N_GRP * N_ROW) // CELL


def mm(a, b, ca=1, cb=0):
    return lax.dot_general(
        a, b, (((ca,), (cb,)), ((), ())), precision=lax.Precision.HIGHEST, preferred_element_type=F32
    )


def split(x):
    hi = x.astype(BF16)
    return hi, (x - hi.astype(F32)).astype(BF16)


def eye16():
    r = lax.broadcasted_iota(jnp.int32, (COLS, COLS), 0)
    c = lax.broadcasted_iota(jnp.int32, (COLS, COLS), 1)
    return (r == c).astype(F32)


def sym(g):
    return 0.5 * (g + g.T)


def eliminate(*systems):
    mats = [jnp.concatenate([s, h], axis=1) for s, h in systems]
    rows = lax.broadcasted_iota(jnp.int32, mats[0].shape, 0)
    for j in range(COLS):
        for n, m in enumerate(mats):
            row = m[j : j + 1, :] / m[j : j + 1, j : j + 1]
            mats[n] = jnp.where(rows == j, row, m - m[:, j : j + 1] * row)
    return [m[:, COLS:] for m in mats]


def flat(v):
    return jnp.concatenate([v[i] for i in range(BR)], axis=1)


def kernel(
    cols_ref, lost_ref, tiles_ref, pre_ref, b_ref, rec_ref, tres_ref,
    stage, zstage, hl, zhl, win, winb, rhs, msg, near, far0, far1, far2, far3, local,
    load_sem, hs_sem, hr_sem, ns_sem, nr_sem, fs_sem, fr_sem,
):
    g = lax.axis_index("grp")
    r = lax.axis_index("row")
    d = g * N_ROW + r
    cell = r // CELL
    pos = lax.rem(r, CELL)
    my_far = g * (N_ROW // CELL) + cell
    first = d * BR - BAND

    def near_dev(n):
        return (g, cell * CELL + lax.rem(pos + n, CELL))

    def far_dev(n):
        f = lax.rem(my_far + n, FAR)
        return (f // (N_ROW // CELL), lax.rem(f, N_ROW // CELL) * CELL + pos)

    def halo_dev(o):
        t = lax.rem(d + o + N_GRP * N_ROW, N_GRP * N_ROW)
        return (t // N_ROW, lax.rem(t, N_ROW))

    offsets = [1, -1, 2, -2, 3, -3]
    fars = [far0, far1, far2, far3]

    for i in range(BR):
        pltpu.make_async_copy(tiles_ref.at[i], stage.at[i], load_sem.at[i]).start()
    pltpu.make_async_copy(pre_ref, zstage, load_sem.at[BR]).start()

    barrier = pltpu.get_barrier_semaphore()
    for o in offsets:
        pl.semaphore_signal(barrier, inc=1, device_id=halo_dev(o), device_id_type=MESH)
    for n in range(1, CELL):
        pl.semaphore_signal(barrier, inc=1, device_id=near_dev(n), device_id_type=MESH)
    for n in range(1, FAR):
        pl.semaphore_signal(barrier, inc=1, device_id=far_dev(n), device_id_type=MESH)
    win[0, BAND : BAND + BR] = b_ref[...]

    def localise(k, carry):
        for i in range(BR):
            local[i, k] = jnp.clip(cols_ref[i, k] - first, 0, WIN - 1)
        return carry

    lax.fori_loop(0, K, localise, 0)
    pl.semaphore_wait(barrier, len(offsets) + CELL - 1 + FAR - 1)

    def halo_send(rd):
        for o in offsets:
            pltpu.make_async_remote_copy(
                src_ref=win.at[rd, pl.ds(BAND, BR)],
                dst_ref=win.at[rd, pl.ds((REACH - o) * BR, BR)],
                send_sem=hs_sem.at[rd],
                recv_sem=hr_sem.at[rd],
                device_id=halo_dev(o),
                device_id_type=MESH,
            ).start()

    def wait_bytes(ref, sem):
        pltpu.make_async_copy(ref, ref, sem).wait()

    def halo_wait(rd):
        wait_bytes(win.at[rd, pl.ds(0, WIN - BR)], hr_sem.at[rd])

    def near_send(gm, value):
        lanes = value.shape[1]
        msg[gm, 0] = jnp.concatenate([value, jnp.zeros((COLS, TB - lanes), F32)], axis=1)
        near[gm, pos] = msg[gm, 0]
        for n in range(1, CELL):
            pltpu.make_async_remote_copy(
                src_ref=msg.at[gm, 0],
                dst_ref=near.at[gm, pos],
                send_sem=ns_sem.at[gm],
                recv_sem=nr_sem.at[gm],
                device_id=near_dev(n),
                device_id_type=MESH,
            ).start()

    def far_send(gm):
        wait_bytes(near.at[gm, pl.ds(0, CELL - 1)], nr_sem.at[gm])
        total = near[gm, 0]
        for n in range(1, CELL):
            total = total + near[gm, n]
        msg[gm, 1] = total
        fars[gm][my_far] = total
        for n in range(1, FAR):
            pltpu.make_async_remote_copy(
                src_ref=msg.at[gm, 1],
                dst_ref=fars[gm].at[my_far],
                send_sem=fs_sem.at[gm],
                recv_sem=fr_sem.at[gm],
                device_id=far_dev(n),
                device_id_type=MESH,
            ).start()

    def far_wait(gm):
        wait_bytes(fars[gm].at[pl.ds(0, FAR - 1)], fr_sem.at[gm])

    def far_all(gm):
        far_wait(gm)
        total = fars[gm][0]
        for n in range(1, FAR):
            total = total + fars[gm][n]
        return total

    lost = lax.rem(lost_ref[0], N_GRP)

    def far_lost(gm):
        far_wait(gm)
        total = fars[gm][lost * (N_ROW // CELL)]
        for n in range(1, N_ROW // CELL):
            total = total + fars[gm][lost * (N_ROW // CELL) + n]
        return total

    def prepare(rd):
        for p in range(2 * REACH + 1):
            group = lax.rem(d + (p - REACH) + N_GRP * N_ROW, N_GRP * N_ROW) // N_ROW
            own = jnp.where(group == g, 1.0, 0.0).astype(F32)
            for q in range(BR):
                x = win[rd, p * BR + q]
                hi, lo = split(x)
                hi_own = hi * own.astype(BF16)
                lo_own = lo * own.astype(BF16)
                winb[p * BR + q] = jnp.concatenate([hi_own, lo_own, hi - hi_own, lo - lo_own], axis=0)

    def product(rd):
        halo_wait(rd)
        prepare(rd)
        own, other = [], []
        for i in range(BR):
            for k in range(K):
                rhs[i, :, k * TB : (k + 1) * TB] = winb[local[i, k]]
            o = lax.dot_general(hl[i], rhs[i], (((1,), (1,)), ((), ())), preferred_element_type=F32)
            o = (o[:TB] + o[TB:]).T
            own.append(o[:COLS] + o[COLS : 2 * COLS])
            other.append(o[2 * COLS : 3 * COLS] + o[3 * COLS :])
        return jnp.concatenate(own, axis=1), jnp.concatenate(other, axis=1)

    def condition(v):
        out = []
        for i in range(BR):
            hi, lo = split(v[:, i * TB : (i + 1) * TB])
            o = lax.dot_general(
                zhl[i], jnp.concatenate([hi, lo], axis=0), (((1,), (1,)), ((), ())), preferred_element_type=F32
            )
            o = (o[:TB] + o[TB:]).T
            out.append(o[:COLS] + o[COLS:])
        return jnp.concatenate(out, axis=1)

    def put(rd, v):
        for i in range(BR):
            win[rd, BAND + i] = v[:, i * TB : (i + 1) * TB]

    def lanes(m, *spans):
        return jnp.concatenate([m[a : a + COLS, b : b + n] for a, b, n in spans], axis=1)

    halo_send(0)
    for i in range(BR):
        pltpu.make_async_copy(tiles_ref.at[i], stage.at[i], load_sem.at[i]).wait()

        def convert(k, carry, i=i):
            hi, lo = split(stage[i, k])
            at = pl.ds(pl.multiple_of(k * TB, TB), TB)
            hl[i, 0:TB, at] = hi
            hl[i, TB : 2 * TB, at] = lo
            return carry

        lax.fori_loop(0, K, convert, 0)
    pltpu.make_async_copy(pre_ref, zstage, load_sem.at[BR]).wait()
    for i in range(BR):
        hi, lo = split(zstage[i])
        zhl[i, 0:TB] = hi
        zhl[i, TB : 2 * TB] = lo
    v0 = flat(b_ref)
    own, p0 = product(0)
    v1 = own + p0 - v0
    put(1, v1)
    halo_send(1)
    basis = jnp.concatenate([v0, v1], axis=0)
    ga = mm(basis, basis, 1, 1)
    near_send(0, lanes(ga, (0, 0, 32), (16, 0, 32)))
    far_send(0)
    own, p1 = product(1)
    v2 = own + p1 - v1
    gb = mm(basis, v2, 1, 1)
    near_send(1, lanes(gb, (0, 0, 16), (16, 0, 16)))
    one = eye16()
    ga = far_all(0)
    ga = jnp.concatenate([ga[:, 0:32], ga[:, 32:64]], axis=0)
    g00 = sym(ga[0:16, 0:16])
    half = sym(ga[0:16, 16:32])
    e0, inv0 = eliminate((g00 + half, half), (g00, one))
    a0 = one - e0
    c = jnp.concatenate([e0, -a0], axis=0)
    squares = mm(c, mm(ga, c), 0, 0)
    m0 = mm(inv0, squares)
    far_send(1)
    d0 = e0 + m0
    d1 = -a0
    dd = jnp.concatenate([d0, d1], axis=0)
    curve = mm(dd, mm(ga, jnp.concatenate([d0, d0 + d1], axis=0)), 0, 0)
    gb = far_all(1)
    gb = jnp.concatenate([gb[:, 0:16], gb[:, 16:32]], axis=0)
    curve = curve + mm(dd, mm(gb, d1), 0, 0)
    (a1,) = eliminate((sym(curve), squares))
    cs = mm(dd, a1) + jnp.concatenate([a0, jnp.zeros_like(a0)], axis=0)
    coupled = mm(cs, jnp.concatenate([p0, p1], axis=0), 0, 0)
    rr = v0 - coupled
    s0 = condition(rr)
    put(2, s0)
    halo_send(2)
    base_rec = mm(cs, basis, 0, 0)
    d0a = mm(d0, a1)
    d1a = mm(d1, a1)
    rc = jnp.concatenate([e0 - d0a, -(a0 + d0a + d1a), -d1a], axis=0)
    residual = mm(rc, jnp.concatenate([v0, v1, v2], axis=0), 0, 0)
    q0, ps0 = product(2)
    t0 = condition(q0)
    put(3, t0)
    halo_send(3)
    g2 = mm(jnp.concatenate([rr, s0, q0], axis=0), jnp.concatenate([s0, q0, t0], axis=0), 1, 1)
    near_send(2, lanes(g2, (0, 0, 16), (0, 32, 16), (16, 16, 16), (32, 32, 16)))
    far_send(2)
    q1, ps1 = product(3)
    st = jnp.concatenate([s0, t0], axis=0)
    g3 = mm(st, q1, 1, 1)
    near_send(3, lanes(g3, (0, 0, 16), (16, 0, 16)))
    g2 = far_lost(2)
    w0 = g2[:, 0:16]
    rt, sq, qt = g2[:, 16:32], g2[:, 32:48], g2[:, 48:64]
    b0, invw = eliminate((sym(sq), w0), (sym(w0), one))
    w1 = w0 - mm(rt, b0) + mm(b0, mm(qt, b0) - sq.T, 0, 0)
    n0 = one + mm(invw, w1)
    far_send(3)
    nb = jnp.concatenate([n0, -b0], axis=0)
    bend = mm(nb, mm(jnp.concatenate([sq, qt.T], axis=0), n0), 0, 0)
    side = jnp.where(r < N_ROW // 2, g - 1, g + 1)
    is_lost = g == lost
    touch = jnp.where(side == lost, 1.0, 0.0).astype(F32)
    base = jnp.where(is_lost, rr, residual + touch * coupled)
    xa = jnp.where(is_lost, q0, touch * ps0)
    xb = jnp.where(is_lost, q1, touch * ps1)
    xs = jnp.concatenate([xa, xb], axis=0)
    g3 = far_lost(3)
    g3 = jnp.concatenate([g3[:, 0:16], g3[:, 16:32]], axis=0)
    bend = bend - mm(nb, mm(g3, b0), 0, 0)
    (b1,) = eliminate((sym(bend), w1))
    es = mm(nb, b1) + jnp.concatenate([b0, jnp.zeros_like(b0)], axis=0)
    rec = jnp.where(is_lost, mm(es, st, 0, 0), base_rec)
    tres = base - mm(es, xs, 0, 0)
    for i in range(BR):
        rec_ref[i] = rec[:, i * TB : (i + 1) * TB]
        tres_ref[i] = tres[:, i * TB : (i + 1) * TB]
    for rd in range(4):
        wait_bytes(win.at[rd, pl.ds(0, WIN - BR)], hs_sem.at[rd])
        wait_bytes(near.at[rd, pl.ds(0, CELL - 1)], ns_sem.at[rd])
        wait_bytes(fars[rd].at[pl.ds(0, FAR - 1)], fs_sem.at[rd])


def per_device(matrix_tiles, column_index, precond, right_side, lost_group):
    vmem = pl.BlockSpec(memory_space=pltpu.VMEM)
    smem = pl.BlockSpec(memory_space=pltpu.SMEM)
    hbm = pl.BlockSpec(memory_space=pl.ANY)
    shape = jax.ShapeDtypeStruct((BR, COLS, TB), F32)
    dma = pltpu.SemaphoreType.DMA
    return pl.pallas_call(
        kernel,
        out_shape=(shape, shape),
        in_specs=[smem, smem, hbm, hbm, vmem],
        out_specs=(vmem, vmem),
        scratch_shapes=[
            pltpu.VMEM((BR, K, TB, TB), F32),
            pltpu.VMEM((BR, TB, TB), F32),
            pltpu.VMEM((BR, 2 * TB, K * TB), BF16),
            pltpu.VMEM((BR, 2 * TB, TB), BF16),
            pltpu.VMEM((4, WIN, COLS, TB), F32),
            pltpu.VMEM((WIN, 4 * COLS, TB), BF16),
            pltpu.VMEM((BR, 4 * COLS, K * TB), BF16),
            pltpu.VMEM((4, 2, COLS, TB), F32),
            pltpu.VMEM((4, CELL, COLS, TB), F32),
            pltpu.VMEM((FAR, COLS, TB), F32),
            pltpu.VMEM((FAR, COLS, TB), F32),
            pltpu.VMEM((FAR, COLS, TB), F32),
            pltpu.VMEM((FAR, COLS, TB), F32),
            pltpu.SMEM((BR, K), jnp.int32),
            dma((BR + 1,)),
            dma((4,)),
            dma((4,)),
            dma((4,)),
            dma((4,)),
            dma((4,)),
            dma((4,)),
        ],
        compiler_params=pltpu.CompilerParams(
            collective_id=0, has_side_effects=True, vmem_limit_bytes=48 * 2**20
        ),
        name="recover",
    )(column_index, lost_group, matrix_tiles, precond, right_side)


def solution(mesh):
    in_specs = (
        P(("grp", "row"), None, None, None),
        P(("grp", "row"), None),
        P(("grp", "row"), None, None),
        P(("grp", "row"), None, None),
        P(),
    )
    out_specs = (P(("grp", "row"), None, None), P(("grp", "row"), None, None))
    return jax.shard_map(
        per_device, mesh=mesh, in_specs=in_specs, out_specs=out_specs, check_vma=False
    )
```

```python
import functools

import jax
import jax.numpy as jnp
from jax import lax
from jax.experimental import pallas as pl
from jax.experimental.pallas import tpu as pltpu
from jax.sharding import PartitionSpec as P

BAND = 12
F32 = jnp.float32
BF16 = jnp.bfloat16
MESH = pl.DeviceIdType.MESH
N_GRP, N_ROW, BR, K, COLS, TB = 4, 32, 4, 32, 16, 128
REACH = 3
WIN = BR * (2 * REACH + 1)
CELL = 8
FAR = (N_GRP * N_ROW) // CELL
CELLS = N_ROW // CELL
WB, WZ, WV, WP, WQ, WT = range(6)
WINS = 6


def mm(a, b, ca=1, cb=0):
    return lax.dot_general(
        a, b, (((ca,), (cb,)), ((), ())), precision=lax.Precision.HIGHEST, preferred_element_type=F32
    )


def split(x):
    hi = x.astype(BF16)
    return hi, (x - hi.astype(F32)).astype(BF16)


def eye16():
    r = lax.broadcasted_iota(jnp.int32, (COLS, COLS), 0)
    c = lax.broadcasted_iota(jnp.int32, (COLS, COLS), 1)
    return (r == c).astype(F32)


def sym(g):
    return 0.5 * (g + g.T)


def eliminate(*systems):
    mats = [jnp.concatenate([s, h], axis=1) for s, h in systems]
    rows = lax.broadcasted_iota(jnp.int32, mats[0].shape, 0)
    for j in range(COLS):
        for n, m in enumerate(mats):
            row = m[j : j + 1, :] / m[j : j + 1, j : j + 1]
            mats[n] = jnp.where(rows == j, row, m - m[:, j : j + 1] * row)
    return [m[:, COLS:] for m in mats]


def flat(v):
    return jnp.concatenate([v[i] for i in range(BR)], axis=1)


def kernel(
    cols_hbm, lost_hbm, tiles_ref, pre_hbm, b_hbm, rec_ref, tres_ref,
    stage, zstage, hl, zhl, win, winb, winc, rhs, msg, near, far0, far1, side2, side3, cols_ref, lost_ref, local,
    load_sem, hs_sem, hr_sem, ns_sem, nr_sem, fs_sem, fr_sem, as_sem, ar_sem,
):
    g = lax.axis_index("grp")
    r = lax.axis_index("row")
    d = g * N_ROW + r
    cell = r // CELL
    pos = lax.rem(r, CELL)
    my_far = g * CELLS + cell
    first = d * BR - BAND
    total_devices = N_GRP * N_ROW

    def near_dev(n):
        return (g, cell * CELL + lax.rem(pos + n, CELL))

    def far_dev(n):
        f = lax.rem(my_far + n, FAR)
        return (f // CELLS, lax.rem(f, CELLS) * CELL + pos)

    def halo_dev(o):
        t = lax.rem(d + o + total_devices, total_devices)
        return (t // N_ROW, lax.rem(t, N_ROW))

    offsets = [3, -3, 2, -2, 1, -1]
    fars = [far0, far1]
    sides = [side2, side3]

    for side in sides:
        for n in range(CELLS):
            side[CELLS + n] = jnp.zeros((COLS, TB), F32)

    barrier = pltpu.get_barrier_semaphore()
    for o in offsets:
        pl.semaphore_signal(barrier, inc=1, device_id=halo_dev(o), device_id_type=MESH)
    for n in range(1, FAR):
        pl.semaphore_signal(barrier, inc=1, device_id=far_dev(n), device_id_type=MESH)
    for n in range(1, CELL):
        pl.semaphore_signal(barrier, inc=1, device_id=near_dev(n), device_id_type=MESH)

    own_span = pl.ds(BAND, BR)
    loads = [
        pltpu.make_async_copy(b_hbm, win.at[WB, own_span], load_sem.at[0]),
        pltpu.make_async_copy(pre_hbm, zstage, load_sem.at[1]),
        pltpu.make_async_copy(cols_hbm, cols_ref, load_sem.at[2]),
        pltpu.make_async_copy(lost_hbm, lost_ref, load_sem.at[3]),
    ] + [pltpu.make_async_copy(tiles_ref.at[i], stage.at[i], load_sem.at[4 + i]) for i in range(BR)]
    for load in loads:
        load.start()

    def wait_bytes(ref, sem):
        pltpu.make_async_copy(ref, ref, sem).wait()

    def halo_send(w):
        for o in offsets:
            pltpu.make_async_remote_copy(
                src_ref=win.at[w, own_span],
                dst_ref=win.at[w, pl.ds((REACH - o) * BR, BR)],
                send_sem=hs_sem.at[w],
                recv_sem=hr_sem.at[w],
                device_id=halo_dev(o),
                device_id_type=MESH,
            ).start()

    def halo_wait(w):
        wait_bytes(win.at[w, pl.ds(0, WIN - BR)], hr_sem.at[w])

    def near_send(gm, value):
        n_lanes = value.shape[1]
        value = jnp.concatenate([value, jnp.zeros((COLS, TB - n_lanes), F32)], axis=1)
        msg[gm, 0] = value
        near[gm, pos] = value
        for n in range(1, CELL):
            pltpu.make_async_remote_copy(
                src_ref=msg.at[gm, 0],
                dst_ref=near.at[gm, pos],
                send_sem=ns_sem.at[gm],
                recv_sem=nr_sem.at[gm],
                device_id=near_dev(n),
                device_id_type=MESH,
            ).start()

    def near_sum(gm):
        wait_bytes(near.at[gm, pl.ds(0, CELL - 1)], nr_sem.at[gm])
        terms = [near[gm, n] for n in range(CELL)]
        while len(terms) > 1:
            terms = [terms[n] + terms[n + 1] for n in range(0, len(terms), 2)]
        msg[gm, 1] = terms[0]
        return terms[0]

    def far_send(gm):
        far = fars[gm]
        far[my_far] = near_sum(gm)
        for n in range(1, FAR):
            pltpu.make_async_remote_copy(
                src_ref=msg.at[gm, 1],
                dst_ref=far.at[my_far],
                send_sem=fs_sem.at[gm],
                recv_sem=fr_sem.at[gm],
                device_id=far_dev(n),
                device_id_type=MESH,
            ).start()

    def far_all(gm):
        far = fars[gm]
        wait_bytes(far.at[pl.ds(0, FAR - 1)], fr_sem.at[gm])
        terms = [far[n] for n in range(FAR)]
        while len(terms) > 1:
            terms = [terms[n] + terms[n + 1] for n in range(0, len(terms), 2)]
        return terms[0]

    def side_send(gm):
        side = sides[gm - 2]
        side[cell] = near_sum(gm)
        for n in range(1, CELLS):
            pltpu.make_async_remote_copy(
                src_ref=msg.at[gm, 1],
                dst_ref=side.at[cell],
                send_sem=fs_sem.at[gm],
                recv_sem=fr_sem.at[gm],
                device_id=(g, lax.rem(cell + n, CELLS) * CELL + pos),
                device_id_type=MESH,
            ).start()
        for step, target in ((1, 0), (N_GRP - 1, CELLS - 1)):
            pltpu.make_async_remote_copy(
                src_ref=msg.at[gm, 1],
                dst_ref=side.at[CELLS + cell],
                send_sem=as_sem.at[gm - 2],
                recv_sem=ar_sem.at[gm - 2],
                device_id=(lax.rem(g + step, N_GRP), target * CELL + pos),
                device_id_type=MESH,
            ).start()

    lost_of = [None]

    def side_sum(gm):
        side = sides[gm - 2]
        wait_bytes(side.at[pl.ds(0, CELLS - 1)], fr_sem.at[gm])

        @pl.when(jnp.logical_or(cell == 0, cell == CELLS - 1))
        def _():
            wait_bytes(side.at[pl.ds(0, CELLS)], ar_sem.at[gm - 2])

        own = (side[0] + side[1]) + (side[2] + side[3])
        other = (side[4] + side[5]) + (side[6] + side[7])
        return jnp.where(lost_of[0], other, own)

    def prepare(w, ref, at):
        for p in range(2 * REACH + 1):
            group = lax.rem(d + (p - REACH) + total_devices, total_devices) // N_ROW
            own = jnp.where(group == g, 1.0, 0.0).astype(BF16)
            for q in range(BR):
                hi, lo = split(win[w, p * BR + q])
                hi_own = hi * own
                lo_own = lo * own
                ref[p * BR + q, at : at + 4 * COLS] = jnp.concatenate(
                    [hi_own, lo_own, hi - hi_own, lo - lo_own], axis=0
                )

    def product(ref, count):
        own = [[] for _ in range(count)]
        other = [[] for _ in range(count)]
        rows = 4 * COLS * count
        for i in range(BR):
            for k in range(K):
                rhs[i, 0:rows, k * TB : (k + 1) * TB] = ref[local[i, k]]
            o = lax.dot_general(hl[i], rhs[i, 0:rows], (((1,), (1,)), ((), ())), preferred_element_type=F32)
            o = (o[:TB] + o[TB:]).T
            for n in range(count):
                own[n].append(o[4 * n * COLS : (4 * n + 1) * COLS] + o[(4 * n + 1) * COLS : (4 * n + 2) * COLS])
                other[n].append(
                    o[(4 * n + 2) * COLS : (4 * n + 3) * COLS] + o[(4 * n + 3) * COLS : (4 * n + 4) * COLS]
                )
        return [jnp.concatenate(v, axis=1) for v in own], [jnp.concatenate(v, axis=1) for v in other]

    def condition(*vectors):
        out = [[] for _ in vectors]
        for i in range(BR):
            parts = []
            for v in vectors:
                parts.extend(split(v[:, i * TB : (i + 1) * TB]))
            o = lax.dot_general(
                zhl[i], jnp.concatenate(parts, axis=0), (((1,), (1,)), ((), ())), preferred_element_type=F32
            )
            o = (o[:TB] + o[TB:]).T
            for n in range(len(vectors)):
                out[n].append(o[2 * n * COLS : (2 * n + 1) * COLS] + o[(2 * n + 1) * COLS : (2 * n + 2) * COLS])
        return [jnp.concatenate(v, axis=1) for v in out]

    def put(w, v):
        for i in range(BR):
            win[w, BAND + i] = v[:, i * TB : (i + 1) * TB]

    def lanes(m, *spans):
        return jnp.concatenate([m[a : a + COLS, b : b + n] for a, b, n in spans], axis=1)

    def stack(*parts):
        return jnp.concatenate(parts, axis=0)

    loads[0].wait()
    pl.semaphore_wait(barrier, len(offsets) + CELL - 1 + FAR - 1)
    halo_send(WB)
    loads[1].wait()
    for i in range(BR):
        hi, lo = split(zstage[i])
        zhl[i, 0:TB] = hi
        zhl[i, TB : 2 * TB] = lo
    v0 = jnp.concatenate([win[WB, BAND + i] for i in range(BR)], axis=1)
    (zb,) = condition(v0)
    put(WZ, zb)
    halo_send(WZ)
    loads[2].wait()

    def localise(k, carry):
        for i in range(BR):
            local[i, k] = jnp.clip(cols_ref[i, k] - first, 0, WIN - 1)
        return carry

    lax.fori_loop(0, K, localise, 0)
    for i in range(BR):
        loads[4 + i].wait()

        def convert(k, carry, i=i):
            hi, lo = split(stage[i, k])
            at = pl.ds(pl.multiple_of(k * TB, TB), TB)
            hl[i, 0:TB, at] = hi
            hl[i, TB : 2 * TB, at] = lo
            return carry

        lax.fori_loop(0, K, convert, 0)
    halo_wait(WB)
    prepare(WB, winb, 0)
    (own,), (p0,) = product(winb, 1)
    v1 = own + p0 - v0
    put(WV, v1)
    halo_send(WV)
    (zp0,) = condition(p0)
    put(WP, zp0)
    halo_send(WP)
    basis = stack(v0, v1)
    ga = mm(basis, basis, 1, 1)
    near_send(0, lanes(ga, (0, 0, 32), (16, 0, 32)))
    loads[3].wait()
    lost = lax.rem(lost_ref[0], N_GRP)
    edge = jnp.logical_or(cell == 0, cell == CELLS - 1)
    touch = jnp.logical_and(edge, jnp.where(r < N_ROW // 2, g - 1, g + 1) == lost)
    is_lost = g == lost
    lost_of[0] = touch
    halo_wait(WZ)
    prepare(WZ, winc, 0)
    far_send(0)
    halo_wait(WV)
    prepare(WV, winb, 0)
    (own,), (p1,) = product(winb, 1)
    (zp1,) = condition(p1)
    put(WQ, zp1)
    halo_send(WQ)
    v2 = own + p1 - v1
    gb = mm(basis, v2, 1, 1)
    near_send(1, lanes(gb, (0, 0, 16), (16, 0, 16)))
    one = eye16()
    ga = far_all(0)
    ga = stack(ga[:, 0:32], ga[:, 32:64])
    g00 = sym(ga[0:16, 0:16])
    half = sym(ga[0:16, 16:32])
    e0, inv0 = eliminate((g00 + half, half), (g00, one))
    a0 = one - e0
    c = stack(e0, -a0)
    squares = mm(c, mm(ga, c), 0, 0)
    far_send(1)
    m0 = mm(inv0, squares)
    d0 = e0 + m0
    d1 = -a0
    dd = stack(d0, d1)
    curve = mm(dd, mm(ga, stack(d0, d0 + d1)), 0, 0)
    halo_wait(WP)
    prepare(WP, winc, 4 * COLS)
    halo_wait(WQ)
    prepare(WQ, winc, 8 * COLS)
    (bz, bzp0, bzp1), (oz, ozp0, ozp1) = product(winc, 3)
    y, yp0, yp1 = condition(bz, bzp0, bzp1)
    gb = far_all(1)
    gb = stack(gb[:, 0:16], gb[:, 16:32])
    curve = curve + mm(dd, mm(gb, d1), 0, 0)
    (a1,) = eliminate((sym(curve), squares))
    cs = mm(dd, a1) + stack(a0, jnp.zeros_like(a0))
    t0 = y - mm(cs, stack(yp0, yp1), 0, 0)
    put(WT, t0)
    halo_send(WT)
    coupled = mm(cs, stack(p0, p1), 0, 0)
    rr = v0 - coupled
    s0 = zb - mm(cs, stack(zp0, zp1), 0, 0)
    q0 = bz - mm(cs, stack(bzp0, bzp1), 0, 0)
    g2 = mm(stack(rr, s0, q0), stack(s0, q0, t0), 1, 1)
    near_send(2, lanes(g2, (0, 0, 16), (0, 32, 16), (16, 16, 16), (32, 32, 16)))
    ps0 = oz - mm(cs, stack(ozp0, ozp1), 0, 0)
    base_rec = mm(cs, basis, 0, 0)
    d0a = mm(d0, a1)
    d1a = mm(d1, a1)
    rc = stack(e0 - d0a, -(a0 + d0a + d1a), -d1a)
    residual = mm(rc, stack(v0, v1, v2), 0, 0)
    st = stack(s0, t0)
    side_send(2)
    halo_wait(WT)
    prepare(WT, winb, 0)
    (q1,), (ps1,) = product(winb, 1)
    g3 = mm(st, q1, 1, 1)
    near_send(3, lanes(g3, (0, 0, 16), (16, 0, 16)))
    g2 = side_sum(2)
    w0 = g2[:, 0:16]
    rt, sq, qt = g2[:, 16:32], g2[:, 32:48], g2[:, 48:64]
    b0, invw = eliminate((sym(sq), w0), (sym(w0), one))
    w1 = w0 - mm(rt, b0) + mm(b0, mm(qt, b0) - sq.T, 0, 0)
    side_send(3)
    n0 = one + mm(invw, w1)
    nb = stack(n0, -b0)
    bend = mm(nb, mm(stack(sq, qt.T), n0), 0, 0)
    base = jnp.where(is_lost, rr, residual + jnp.where(touch, coupled, 0.0))
    xs = stack(jnp.where(is_lost, q0, ps0), jnp.where(is_lost, q1, ps1))
    g3 = side_sum(3)
    g3 = stack(g3[:, 0:16], g3[:, 16:32])
    bend = bend - mm(nb, mm(g3, b0), 0, 0)
    (b1,) = eliminate((sym(bend), w1))
    es = mm(nb, b1) + stack(b0, jnp.zeros_like(b0))
    rec = jnp.where(is_lost, mm(es, st, 0, 0), base_rec)
    tres = jnp.where(jnp.logical_or(is_lost, touch), base - mm(es, xs, 0, 0), base)
    for i in range(BR):
        rec_ref[i] = rec[:, i * TB : (i + 1) * TB]
        tres_ref[i] = tres[:, i * TB : (i + 1) * TB]
    for w in range(WINS):
        wait_bytes(win.at[w, pl.ds(0, WIN - BR)], hs_sem.at[w])
    for gm in range(4):
        wait_bytes(near.at[gm, pl.ds(0, CELL - 1)], ns_sem.at[gm])
    for gm in range(2):
        wait_bytes(fars[gm].at[pl.ds(0, FAR - 1)], fs_sem.at[gm])
        wait_bytes(sides[gm].at[pl.ds(0, CELLS - 1)], fs_sem.at[gm + 2])
        wait_bytes(sides[gm].at[pl.ds(0, 2)], as_sem.at[gm])


def per_device(matrix_tiles, column_index, precond, right_side, lost_group):
    vmem = pl.BlockSpec(memory_space=pltpu.VMEM)
    hbm = pl.BlockSpec(memory_space=pltpu.HBM)
    shape = jax.ShapeDtypeStruct((BR, COLS, TB), F32)
    dma = pltpu.SemaphoreType.DMA
    return pl.pallas_call(
        kernel,
        out_shape=(shape, shape),
        in_specs=[hbm, hbm, hbm, hbm, hbm],
        out_specs=(vmem, vmem),
        scratch_shapes=[
            pltpu.VMEM((BR, K, TB, TB), F32),
            pltpu.VMEM((BR, TB, TB), F32),
            pltpu.VMEM((BR, 2 * TB, K * TB), BF16),
            pltpu.VMEM((BR, 2 * TB, TB), BF16),
            pltpu.VMEM((WINS, WIN, COLS, TB), F32),
            pltpu.VMEM((WIN, 4 * COLS, TB), BF16),
            pltpu.VMEM((WIN, 12 * COLS, TB), BF16),
            pltpu.VMEM((BR, 12 * COLS, K * TB), BF16),
            pltpu.VMEM((4, 2, COLS, TB), F32),
            pltpu.VMEM((4, CELL, COLS, TB), F32),
            pltpu.VMEM((FAR, COLS, TB), F32),
            pltpu.VMEM((FAR, COLS, TB), F32),
            pltpu.VMEM((2 * CELLS, COLS, TB), F32),
            pltpu.VMEM((2 * CELLS, COLS, TB), F32),
            pltpu.SMEM((BR, K), jnp.int32),
            pltpu.SMEM((1,), jnp.int32),
            pltpu.SMEM((BR, K), jnp.int32),
            dma((4 + BR,)),
            dma((WINS,)),
            dma((WINS,)),
            dma((4,)),
            dma((4,)),
            dma((4,)),
            dma((4,)),
            dma((2,)),
            dma((2,)),
        ],
        compiler_params=pltpu.CompilerParams(
            collective_id=0, has_side_effects=True, vmem_limit_bytes=int(64 * 2**20)
        ),
        name="recover",
    )(column_index, lost_group, matrix_tiles, precond, right_side)


def solution(mesh):
    in_specs = (
        P(("grp", "row"), None, None, None),
        P(("grp", "row"), None),
        P(("grp", "row"), None, None),
        P(("grp", "row"), None, None),
        P(),
    )
    out_specs = (P(("grp", "row"), None, None), P(("grp", "row"), None, None))
    return jax.shard_map(
        per_device, mesh=mesh, in_specs=in_specs, out_specs=out_specs, check_vma=False
    )
```

```python
import functools

import jax
import jax.numpy as jnp
from jax import lax
from jax.experimental import pallas as pl
from jax.experimental.pallas import tpu as pltpu
from jax.sharding import PartitionSpec as P

BAND = 12
F32 = jnp.float32
BF16 = jnp.bfloat16
MESH = pl.DeviceIdType.MESH
N_GRP, N_ROW, BR, K, COLS, TB = 4, 32, 4, 32, 16, 128
REACH = 3
WIN = BR * (2 * REACH + 1)
CELL = 8
FAR = (N_GRP * N_ROW) // CELL
CELLS = N_ROW // CELL
WB, WZ, WV, WP, WQ, WT = range(6)
WINS = 6


def mm(a, b, ca=1, cb=0):
    return lax.dot_general(
        a, b, (((ca,), (cb,)), ((), ())), precision=lax.Precision.HIGHEST, preferred_element_type=F32
    )


def split(x):
    hi = x.astype(BF16)
    return hi, (x - hi.astype(F32)).astype(BF16)


def eye16():
    r = lax.broadcasted_iota(jnp.int32, (COLS, COLS), 0)
    c = lax.broadcasted_iota(jnp.int32, (COLS, COLS), 1)
    return (r == c).astype(F32)


def sym(g):
    return 0.5 * (g + g.T)


def eliminate(*systems):
    mats = [jnp.concatenate([s, h], axis=1) for s, h in systems]
    shape = mats[0].shape
    rows = lax.broadcasted_iota(jnp.int32, shape, 0)
    columns = [[jnp.broadcast_to(m[:, j : j + 1], shape) for j in range(COLS)] for m in mats]

    def step(value, column, inverse, j):
        row = value[j : j + 1] * inverse
        return jnp.where(rows == j, row, value - column * row)

    for j in range(COLS):
        for n in range(len(mats)):
            column = columns[n][j]
            inverse = 1.0 / column[j : j + 1]
            mats[n] = step(mats[n], column, inverse, j)
            for u in range(j + 1, COLS):
                columns[n][u] = step(columns[n][u], column, inverse, j)
    return [m[:, COLS:] for m in mats]


def kernel(
    cols_hbm, lost_hbm, tiles_ref, pre_hbm, b_hbm, rec_ref, tres_ref,
    stage, zstage, hl, zhl, win, winb, winc, rhs, msg, near, far0, far1, side, shot, shot_msg, cols_ref, lost_ref, local,
    load_sem, hs_sem, hr_sem, ns_sem, nr_sem, fs_sem, fr_sem, as_sem, ar_sem,
):
    g = lax.axis_index("grp")
    r = lax.axis_index("row")
    d = g * N_ROW + r
    cell = r // CELL
    pos = lax.rem(r, CELL)
    my_far = g * CELLS + cell
    first = d * BR - BAND
    total_devices = N_GRP * N_ROW

    def near_dev(n):
        return (g, cell * CELL + lax.rem(pos + n, CELL))

    def far_dev(n):
        f = lax.rem(my_far + n, FAR)
        return (f // CELLS, lax.rem(f, CELLS) * CELL + pos)

    def halo_dev(o):
        t = lax.rem(d + o + total_devices, total_devices)
        return (t // N_ROW, lax.rem(t, N_ROW))

    border = jnp.logical_or(r < REACH, r >= N_ROW - REACH)
    offsets = [3, -3, 2, -2, 1, -1]
    fars = [far0, far1]

    for n in range(CELLS):
        side[CELLS + n] = jnp.zeros((COLS, TB), F32)
    for n in range(N_ROW):
        shot[N_ROW + n] = jnp.zeros((COLS // 2, TB), F32)

    barrier = pltpu.get_barrier_semaphore()
    for o in offsets:
        pl.semaphore_signal(barrier, inc=1, device_id=halo_dev(o), device_id_type=MESH)
    for n in range(1, FAR):
        pl.semaphore_signal(barrier, inc=1, device_id=far_dev(n), device_id_type=MESH)
    for n in range(1, CELL):
        pl.semaphore_signal(barrier, inc=1, device_id=near_dev(n), device_id_type=MESH)

    own_span = pl.ds(BAND, BR)
    loads = [
        pltpu.make_async_copy(b_hbm, win.at[WB, own_span], load_sem.at[0]),
        pltpu.make_async_copy(pre_hbm, zstage, load_sem.at[1]),
        pltpu.make_async_copy(cols_hbm, cols_ref, load_sem.at[2]),
        pltpu.make_async_copy(lost_hbm, lost_ref, load_sem.at[3]),
    ] + [pltpu.make_async_copy(tiles_ref.at[i], stage.at[i], load_sem.at[4 + i]) for i in range(BR)]
    for load in loads:
        load.start()

    def wait_bytes(ref, sem):
        pltpu.make_async_copy(ref, ref, sem).wait()

    def halo_send(w):
        for o in offsets:
            pltpu.make_async_remote_copy(
                src_ref=win.at[w, own_span],
                dst_ref=win.at[w, pl.ds((REACH - o) * BR, BR)],
                send_sem=hs_sem.at[w],
                recv_sem=hr_sem.at[w],
                device_id=halo_dev(o),
                device_id_type=MESH,
            ).start()

    def halo_wait(w):
        wait_bytes(win.at[w, pl.ds(0, WIN - BR)], hr_sem.at[w])

    def near_send(gm, value):
        n_lanes = value.shape[1]
        value = jnp.concatenate([value, jnp.zeros((COLS, TB - n_lanes), F32)], axis=1)
        msg[gm, 0] = value
        near[gm, pos] = value
        for n in range(1, CELL):
            pltpu.make_async_remote_copy(
                src_ref=msg.at[gm, 0],
                dst_ref=near.at[gm, pos],
                send_sem=ns_sem.at[gm],
                recv_sem=nr_sem.at[gm],
                device_id=near_dev(n),
                device_id_type=MESH,
            ).start()

    def near_sum(gm):
        wait_bytes(near.at[gm, pl.ds(0, CELL - 1)], nr_sem.at[gm])
        terms = [near[gm, n] for n in range(CELL)]
        while len(terms) > 1:
            terms = [terms[n] + terms[n + 1] for n in range(0, len(terms), 2)]
        msg[gm, 1] = terms[0]
        return terms[0]

    def far_send(gm):
        far = fars[gm]
        far[my_far] = near_sum(gm)
        for n in range(1, FAR):
            pltpu.make_async_remote_copy(
                src_ref=msg.at[gm, 1],
                dst_ref=far.at[my_far],
                send_sem=fs_sem.at[gm],
                recv_sem=fr_sem.at[gm],
                device_id=far_dev(n),
                device_id_type=MESH,
            ).start()

    def far_all(gm):
        far = fars[gm]
        wait_bytes(far.at[pl.ds(0, FAR - 1)], fr_sem.at[gm])
        terms = [far[n] for n in range(FAR)]
        while len(terms) > 1:
            terms = [terms[n] + terms[n + 1] for n in range(0, len(terms), 2)]
        return terms[0]

    def side_send(gm):
        side[cell] = near_sum(gm)
        for n in range(1, CELLS):
            pltpu.make_async_remote_copy(
                src_ref=msg.at[gm, 1],
                dst_ref=side.at[cell],
                send_sem=fs_sem.at[gm],
                recv_sem=fr_sem.at[gm],
                device_id=(g, lax.rem(cell + n, CELLS) * CELL + pos),
                device_id_type=MESH,
            ).start()
        for step, target in ((1, 0), (N_GRP - 1, CELLS - 1)):
            pltpu.make_async_remote_copy(
                src_ref=msg.at[gm, 1],
                dst_ref=side.at[CELLS + cell],
                send_sem=as_sem.at[0],
                recv_sem=ar_sem.at[0],
                device_id=(lax.rem(g + step, N_GRP), target * CELL + pos),
                device_id_type=MESH,
            ).start()

    lost_of = [None]

    def side_sum(gm):
        wait_bytes(side.at[pl.ds(0, CELLS - 1)], fr_sem.at[gm])

        @pl.when(jnp.logical_or(cell == 0, cell == CELLS - 1))
        def _():
            wait_bytes(side.at[pl.ds(0, CELLS)], ar_sem.at[0])

        own = (side[0] + side[1]) + (side[2] + side[3])
        other = (side[4] + side[5]) + (side[6] + side[7])
        return jnp.where(lost_of[0], other, own)

    far_edges = [(1, 0), (1, 1), (1, 2), (N_GRP - 1, N_ROW - 1), (N_GRP - 1, N_ROW - 2), (N_GRP - 1, N_ROW - 3)]

    def shot_send(value):
        half = COLS // 2
        parts = [value[n * half : (n + 1) * half] for n in range(4)] + [jnp.zeros((half, TB - 4 * COLS), F32)]
        value = jnp.concatenate(parts, axis=1)
        shot_msg[...] = value
        shot[r] = value
        for n in range(1, N_ROW):
            pltpu.make_async_remote_copy(
                src_ref=shot_msg,
                dst_ref=shot.at[r],
                send_sem=fs_sem.at[3],
                recv_sem=fr_sem.at[3],
                device_id=(g, lax.rem(r + n, N_ROW)),
                device_id_type=MESH,
            ).start()
        for step, target in far_edges:
            pltpu.make_async_remote_copy(
                src_ref=shot_msg,
                dst_ref=shot.at[N_ROW + r],
                send_sem=as_sem.at[1],
                recv_sem=ar_sem.at[1],
                device_id=(lax.rem(g + step, N_GRP), target),
                device_id_type=MESH,
            ).start()

    def shot_sum():
        wait_bytes(shot.at[pl.ds(0, N_ROW - 1)], fr_sem.at[3])

        @pl.when(border)
        def _():
            wait_bytes(shot.at[pl.ds(0, N_ROW)], ar_sem.at[1])

        sums = []
        for at in (0, N_ROW):
            terms = [shot[at + n] for n in range(N_ROW)]
            while len(terms) > 1:
                terms = [terms[n] + terms[n + 1] for n in range(0, len(terms), 2)]
            sums.append(terms[0])
        total = jnp.where(lost_of[0], sums[1], sums[0])
        return jnp.concatenate([total[:, n * COLS : (n + 1) * COLS] for n in range(4)], axis=0)

    def prepare(w, ref, at):
        for p in range(2 * REACH + 1):
            group = lax.rem(d + (p - REACH) + total_devices, total_devices) // N_ROW
            own = jnp.where(group == g, 1.0, 0.0).astype(BF16)
            for q in range(BR):
                hi, lo = split(win[w, p * BR + q])
                hi_own = hi * own
                lo_own = lo * own
                ref[p * BR + q, at : at + 4 * COLS] = jnp.concatenate(
                    [hi_own, lo_own, hi - hi_own, lo - lo_own], axis=0
                )

    def product(ref, count):
        own = [[] for _ in range(count)]
        other = [[] for _ in range(count)]
        rows = 4 * COLS * count
        for i in range(BR):
            for k in range(K):
                rhs[i, 0:rows, k * TB : (k + 1) * TB] = ref[local[i, k]]
            o = lax.dot_general(hl[i], rhs[i, 0:rows], (((1,), (1,)), ((), ())), preferred_element_type=F32)
            o = (o[:TB] + o[TB:]).T
            for n in range(count):
                own[n].append(o[4 * n * COLS : (4 * n + 1) * COLS] + o[(4 * n + 1) * COLS : (4 * n + 2) * COLS])
                other[n].append(
                    o[(4 * n + 2) * COLS : (4 * n + 3) * COLS] + o[(4 * n + 3) * COLS : (4 * n + 4) * COLS]
                )
        return [jnp.concatenate(v, axis=1) for v in own], [jnp.concatenate(v, axis=1) for v in other]

    def condition(*vectors):
        out = [[] for _ in vectors]
        for i in range(BR):
            parts = []
            for v in vectors:
                parts.extend(split(v[:, i * TB : (i + 1) * TB]))
            o = lax.dot_general(
                zhl[i], jnp.concatenate(parts, axis=0), (((1,), (1,)), ((), ())), preferred_element_type=F32
            )
            o = (o[:TB] + o[TB:]).T
            for n in range(len(vectors)):
                out[n].append(o[2 * n * COLS : (2 * n + 1) * COLS] + o[(2 * n + 1) * COLS : (2 * n + 2) * COLS])
        return [jnp.concatenate(v, axis=1) for v in out]

    def put(w, v):
        for i in range(BR):
            win[w, BAND + i] = v[:, i * TB : (i + 1) * TB]

    def lanes(m, *spans):
        return jnp.concatenate([m[a : a + COLS, b : b + n] for a, b, n in spans], axis=1)

    def stack(*parts):
        return jnp.concatenate(parts, axis=0)

    loads[0].wait()
    pl.semaphore_wait(barrier, len(offsets) + CELL - 1 + FAR - 1)
    halo_send(WB)
    loads[1].wait()
    for i in range(BR):
        hi, lo = split(zstage[i])
        zhl[i, 0:TB] = hi
        zhl[i, TB : 2 * TB] = lo
    v0 = jnp.concatenate([win[WB, BAND + i] for i in range(BR)], axis=1)
    (zb,) = condition(v0)
    put(WZ, zb)
    halo_send(WZ)
    loads[2].wait()

    def localise(k, carry):
        for i in range(BR):
            local[i, k] = jnp.clip(cols_ref[i, k] - first, 0, WIN - 1)
        return carry

    lax.fori_loop(0, K, localise, 0)
    for i in range(BR):
        loads[4 + i].wait()

        def convert(k, carry, i=i):
            hi, lo = split(stage[i, k])
            at = pl.ds(pl.multiple_of(k * TB, TB), TB)
            hl[i, 0:TB, at] = hi
            hl[i, TB : 2 * TB, at] = lo
            return carry

        lax.fori_loop(0, K, convert, 0)
    halo_wait(WB)
    prepare(WB, winb, 0)
    (own,), (p0,) = product(winb, 1)
    v1 = own + p0 - v0
    put(WV, v1)
    halo_send(WV)
    (zp0,) = condition(p0)
    put(WP, zp0)
    halo_send(WP)
    basis = stack(v0, v1)
    ga = mm(basis, basis, 1, 1)
    near_send(0, lanes(ga, (0, 0, 32), (16, 0, 32)))
    loads[3].wait()
    lost = lax.rem(lost_ref[0], N_GRP)
    touch = jnp.logical_and(border, jnp.where(r < N_ROW // 2, g - 1, g + 1) == lost)
    is_lost = g == lost
    lost_of[0] = touch
    halo_wait(WZ)
    prepare(WZ, winc, 0)
    far_send(0)
    halo_wait(WV)
    prepare(WV, winb, 0)
    (own,), (p1,) = product(winb, 1)
    (zp1,) = condition(p1)
    put(WQ, zp1)
    halo_send(WQ)
    v2 = own + p1 - v1
    gb = mm(basis, v2, 1, 1)
    near_send(1, lanes(gb, (0, 0, 16), (16, 0, 16)))
    one = eye16()
    ga = far_all(0)
    ga = stack(ga[:, 0:32], ga[:, 32:64])
    g00 = sym(ga[0:16, 0:16])
    half = sym(ga[0:16, 16:32])
    e0, inv0 = eliminate((g00 + half, half), (g00, one))
    a0 = one - e0
    c = stack(e0, -a0)
    squares = mm(c, mm(ga, c), 0, 0)
    far_send(1)
    m0 = mm(inv0, squares)
    d0 = e0 + m0
    d1 = -a0
    dd = stack(d0, d1)
    curve = mm(dd, mm(ga, stack(d0, d0 + d1)), 0, 0)
    halo_wait(WP)
    prepare(WP, winc, 4 * COLS)
    halo_wait(WQ)
    prepare(WQ, winc, 8 * COLS)
    (bz, bzp0, bzp1), (oz, ozp0, ozp1) = product(winc, 3)
    y, yp0, yp1 = condition(bz, bzp0, bzp1)
    gb = far_all(1)
    gb = stack(gb[:, 0:16], gb[:, 16:32])
    curve = curve + mm(dd, mm(gb, d1), 0, 0)
    (a1,) = eliminate((sym(curve), squares))
    cs = mm(dd, a1) + stack(a0, jnp.zeros_like(a0))
    t0 = y - mm(cs, stack(yp0, yp1), 0, 0)
    put(WT, t0)
    halo_send(WT)
    coupled = mm(cs, stack(p0, p1), 0, 0)
    rr = v0 - coupled
    s0 = zb - mm(cs, stack(zp0, zp1), 0, 0)
    q0 = bz - mm(cs, stack(bzp0, bzp1), 0, 0)
    g2 = mm(stack(rr, s0, q0), stack(s0, q0, t0), 1, 1)
    near_send(2, lanes(g2, (0, 0, 16), (0, 32, 16), (16, 16, 16), (32, 32, 16)))
    ps0 = oz - mm(cs, stack(ozp0, ozp1), 0, 0)
    base_rec = mm(cs, basis, 0, 0)
    d0a = mm(d0, a1)
    d1a = mm(d1, a1)
    rc = stack(e0 - d0a, -(a0 + d0a + d1a), -d1a)
    residual = mm(rc, stack(v0, v1, v2), 0, 0)
    st = stack(s0, t0)
    side_send(2)
    halo_wait(WT)
    prepare(WT, winb, 0)
    (q1,), (ps1,) = product(winb, 1)
    g3 = mm(st, q1, 1, 1)
    shot_send(g3)
    g2 = side_sum(2)
    w0 = g2[:, 0:16]
    rt, sq, qt = g2[:, 16:32], g2[:, 32:48], g2[:, 48:64]
    b0, invw = eliminate((sym(sq), w0), (sym(w0), one))
    w1 = w0 - mm(rt, b0) + mm(b0, mm(qt, b0) - sq.T, 0, 0)
    n0 = one + mm(invw, w1)
    nb = stack(n0, -b0)
    bend = mm(nb, mm(stack(sq, qt.T), n0), 0, 0)
    base = jnp.where(is_lost, rr, residual + jnp.where(touch, coupled, 0.0))
    xs = stack(jnp.where(is_lost, q0, ps0), jnp.where(is_lost, q1, ps1))
    g3 = shot_sum()
    bend = bend - mm(nb, mm(g3, b0), 0, 0)
    (b1,) = eliminate((sym(bend), w1))
    es = mm(nb, b1) + stack(b0, jnp.zeros_like(b0))
    rec = jnp.where(is_lost, mm(es, st, 0, 0), base_rec)
    tres = jnp.where(jnp.logical_or(is_lost, touch), base - mm(es, xs, 0, 0), base)
    for i in range(BR):
        rec_ref[i] = rec[:, i * TB : (i + 1) * TB]
        tres_ref[i] = tres[:, i * TB : (i + 1) * TB]
    for w in range(WINS):
        wait_bytes(win.at[w, pl.ds(0, WIN - BR)], hs_sem.at[w])
    for gm in range(3):
        wait_bytes(near.at[gm, pl.ds(0, CELL - 1)], ns_sem.at[gm])
    for gm in range(2):
        wait_bytes(fars[gm].at[pl.ds(0, FAR - 1)], fs_sem.at[gm])
    wait_bytes(side.at[pl.ds(0, CELLS - 1)], fs_sem.at[2])
    wait_bytes(side.at[pl.ds(0, 2)], as_sem.at[0])
    wait_bytes(shot.at[pl.ds(0, N_ROW - 1)], fs_sem.at[3])
    wait_bytes(shot.at[pl.ds(0, len(far_edges))], as_sem.at[1])


def per_device(matrix_tiles, column_index, precond, right_side, lost_group):
    vmem = pl.BlockSpec(memory_space=pltpu.VMEM)
    hbm = pl.BlockSpec(memory_space=pltpu.HBM)
    shape = jax.ShapeDtypeStruct((BR, COLS, TB), F32)
    dma = pltpu.SemaphoreType.DMA
    return pl.pallas_call(
        kernel,
        out_shape=(shape, shape),
        in_specs=[hbm, hbm, hbm, hbm, hbm],
        out_specs=(vmem, vmem),
        scratch_shapes=[
            pltpu.VMEM((BR, K, TB, TB), F32),
            pltpu.VMEM((BR, TB, TB), F32),
            pltpu.VMEM((BR, 2 * TB, K * TB), BF16),
            pltpu.VMEM((BR, 2 * TB, TB), BF16),
            pltpu.VMEM((WINS, WIN, COLS, TB), F32),
            pltpu.VMEM((WIN, 4 * COLS, TB), BF16),
            pltpu.VMEM((WIN, 12 * COLS, TB), BF16),
            pltpu.VMEM((BR, 12 * COLS, K * TB), BF16),
            pltpu.VMEM((3, 2, COLS, TB), F32),
            pltpu.VMEM((3, CELL, COLS, TB), F32),
            pltpu.VMEM((FAR, COLS, TB), F32),
            pltpu.VMEM((FAR, COLS, TB), F32),
            pltpu.VMEM((2 * CELLS, COLS, TB), F32),
            pltpu.VMEM((2 * N_ROW, COLS // 2, TB), F32),
            pltpu.VMEM((COLS // 2, TB), F32),
            pltpu.SMEM((BR, K), jnp.int32),
            pltpu.SMEM((1,), jnp.int32),
            pltpu.SMEM((BR, K), jnp.int32),
            dma((4 + BR,)),
            dma((WINS,)),
            dma((WINS,)),
            dma((3,)),
            dma((3,)),
            dma((4,)),
            dma((4,)),
            dma((2,)),
            dma((2,)),
        ],
        compiler_params=pltpu.CompilerParams(
            collective_id=0, has_side_effects=True, vmem_limit_bytes=55136 * 1024
        ),
        name="recover",
    )(column_index, lost_group, matrix_tiles, precond, right_side)


def solution(mesh):
    in_specs = (
        P(("grp", "row"), None, None, None),
        P(("grp", "row"), None),
        P(("grp", "row"), None, None),
        P(("grp", "row"), None, None),
        P(),
    )
    out_specs = (P(("grp", "row"), None, None), P(("grp", "row"), None, None))
    return jax.shard_map(
        per_device, mesh=mesh, in_specs=in_specs, out_specs=out_specs, check_vma=False
    )
```

```python
import functools

import jax
import jax.numpy as jnp
from jax import lax
from jax.experimental import pallas as pl
from jax.experimental.pallas import tpu as pltpu
from jax.sharding import PartitionSpec as P

BAND = 12
F32 = jnp.float32
BF16 = jnp.bfloat16
MESH = pl.DeviceIdType.MESH
N_GRP, N_ROW, BR, K, COLS, TB = 4, 32, 4, 32, 16, 128
REACH = 3
WIN = BR * (2 * REACH + 1)
CELL = 8
FAR = (N_GRP * N_ROW) // CELL
CELLS = N_ROW // CELL
WB, WZ, WV, WP, WQ, WT = range(6)
WINS = 6


def mm(a, b, ca=1, cb=0):
    return lax.dot_general(
        a, b, (((ca,), (cb,)), ((), ())), precision=lax.Precision.HIGHEST, preferred_element_type=F32
    )


def split(x):
    hi = x.astype(BF16)
    return hi, (x - hi.astype(F32)).astype(BF16)


def eye16():
    r = lax.broadcasted_iota(jnp.int32, (COLS, COLS), 0)
    c = lax.broadcasted_iota(jnp.int32, (COLS, COLS), 1)
    return (r == c).astype(F32)


def sym(g):
    return 0.5 * (g + g.T)


def eliminate(*systems):
    mats = [jnp.concatenate([s, h], axis=1) for s, h in systems]
    shape = mats[0].shape
    rows = lax.broadcasted_iota(jnp.int32, shape, 0)
    columns = [[jnp.broadcast_to(m[:, j : j + 1], shape) for j in range(COLS)] for m in mats]

    def step(value, column, inverse, j):
        row = value[j : j + 1] * inverse
        return jnp.where(rows == j, row, value - column * row)

    for j in range(COLS):
        for n in range(len(mats)):
            column = columns[n][j]
            inverse = 1.0 / column[j : j + 1]
            mats[n] = step(mats[n], column, inverse, j)
            for u in range(j + 1, COLS):
                columns[n][u] = step(columns[n][u], column, inverse, j)
    return [m[:, COLS:] for m in mats]


def kernel(
    cols_hbm, lost_hbm, tiles_ref, pre_hbm, b_hbm, rec_ref, tres_ref,
    stage, zstage, hl, zhl, win, winb, winc, rhs, msg0, msg1, msg2, near0, near1, near2, far0, far1, side, shot, shot_msg, cols_ref, lost_ref, local,
    load_sem, hs_sem, hr_sem, ns_sem, nr_sem, fs_sem, fr_sem, as_sem, ar_sem,
):
    g = lax.axis_index("grp")
    r = lax.axis_index("row")
    d = g * N_ROW + r
    cell = r // CELL
    pos = lax.rem(r, CELL)
    my_far = g * CELLS + cell
    first = d * BR - BAND
    total_devices = N_GRP * N_ROW

    def near_dev(n):
        return (g, cell * CELL + lax.rem(pos + n, CELL))

    def far_dev(n):
        f = lax.rem(my_far + n, FAR)
        return (f // CELLS, lax.rem(f, CELLS) * CELL + pos)

    def halo_dev(o):
        t = lax.rem(d + o + total_devices, total_devices)
        return (t // N_ROW, lax.rem(t, N_ROW))

    border = jnp.logical_or(r < REACH, r >= N_ROW - REACH)
    offsets = [3, -3, 2, -2, 1, -1]
    fars = [far0, far1]
    nears = [near0, near1, near2]
    msgs = [msg0, msg1, msg2]

    barrier = pltpu.get_barrier_semaphore()
    for o in offsets:
        pl.semaphore_signal(barrier, inc=1, device_id=halo_dev(o), device_id_type=MESH)
    for n in range(1, FAR):
        pl.semaphore_signal(barrier, inc=1, device_id=far_dev(n), device_id_type=MESH)
    for n in range(1, CELL):
        pl.semaphore_signal(barrier, inc=1, device_id=near_dev(n), device_id_type=MESH)

    own_span = pl.ds(BAND, BR)
    loads = [
        pltpu.make_async_copy(b_hbm, win.at[WB, own_span], load_sem.at[0]),
        pltpu.make_async_copy(pre_hbm, zstage, load_sem.at[1]),
        pltpu.make_async_copy(cols_hbm, cols_ref, load_sem.at[2]),
        pltpu.make_async_copy(lost_hbm, lost_ref, load_sem.at[3]),
    ] + [pltpu.make_async_copy(tiles_ref.at[i], stage.at[i], load_sem.at[4 + i]) for i in range(BR)]
    for load in loads:
        load.start()

    def wait_bytes(ref, sem):
        pltpu.make_async_copy(ref, ref, sem).wait()

    def halo_send(w):
        for o in offsets:
            pltpu.make_async_remote_copy(
                src_ref=win.at[w, own_span],
                dst_ref=win.at[w, pl.ds((REACH - o) * BR, BR)],
                send_sem=hs_sem.at[w],
                recv_sem=hr_sem.at[w],
                device_id=halo_dev(o),
                device_id_type=MESH,
            ).start()

    def halo_wait(w):
        wait_bytes(win.at[w, pl.ds(0, WIN - BR)], hr_sem.at[w])

    def near_send(gm, value):
        msg, near = msgs[gm], nears[gm]
        n_lanes = value.shape[1]
        value = jnp.concatenate([value, jnp.zeros((value.shape[0], TB - n_lanes), F32)], axis=1)
        msg[0] = value
        near[pos] = value
        for n in range(1, CELL):
            pltpu.make_async_remote_copy(
                src_ref=msg.at[0],
                dst_ref=near.at[pos],
                send_sem=ns_sem.at[gm],
                recv_sem=nr_sem.at[gm],
                device_id=near_dev(n),
                device_id_type=MESH,
            ).start()

    def near_sum(gm):
        msg, near = msgs[gm], nears[gm]
        wait_bytes(near.at[pl.ds(0, CELL - 1)], nr_sem.at[gm])
        terms = [near[n] for n in range(CELL)]
        while len(terms) > 1:
            terms = [terms[n] + terms[n + 1] for n in range(0, len(terms), 2)]
        msg[1] = terms[0]
        return terms[0]

    def far_send(gm):
        far = fars[gm]
        far[my_far] = near_sum(gm)
        for n in range(1, FAR):
            pltpu.make_async_remote_copy(
                src_ref=msgs[gm].at[1],
                dst_ref=far.at[my_far],
                send_sem=fs_sem.at[gm],
                recv_sem=fr_sem.at[gm],
                device_id=far_dev(n),
                device_id_type=MESH,
            ).start()

    def far_all(gm):
        far = fars[gm]
        wait_bytes(far.at[pl.ds(0, FAR - 1)], fr_sem.at[gm])
        terms = [far[n] for n in range(FAR)]
        while len(terms) > 1:
            terms = [terms[n] + terms[n + 1] for n in range(0, len(terms), 2)]
        return terms[0]

    def side_send(gm):
        side[cell] = near_sum(gm)
        for n in range(1, CELLS):
            pltpu.make_async_remote_copy(
                src_ref=msgs[gm].at[1],
                dst_ref=side.at[cell],
                send_sem=fs_sem.at[gm],
                recv_sem=fr_sem.at[gm],
                device_id=(g, lax.rem(cell + n, CELLS) * CELL + pos),
                device_id_type=MESH,
            ).start()
        for step, target in ((1, 0), (N_GRP - 1, CELLS - 1)):
            pltpu.make_async_remote_copy(
                src_ref=msgs[gm].at[1],
                dst_ref=side.at[CELLS + cell],
                send_sem=as_sem.at[0],
                recv_sem=ar_sem.at[0],
                device_id=(lax.rem(g + step, N_GRP), target * CELL + pos),
                device_id_type=MESH,
            ).start()

    lost_of = [None]

    def side_sum(gm):
        wait_bytes(side.at[pl.ds(0, CELLS - 1)], fr_sem.at[gm])

        @pl.when(jnp.logical_or(cell == 0, cell == CELLS - 1))
        def _():
            wait_bytes(side.at[pl.ds(0, CELLS)], ar_sem.at[0])

        own = (side[0] + side[1]) + (side[2] + side[3])
        other = (side[4] + side[5]) + (side[6] + side[7])
        return jnp.where(lost_of[0], other, own)

    far_edges = [(1, 0), (1, 1), (1, 2), (N_GRP - 1, N_ROW - 1), (N_GRP - 1, N_ROW - 2), (N_GRP - 1, N_ROW - 3)]

    def folded(value):
        half = COLS // 2
        return jnp.concatenate([value[n * half : (n + 1) * half] for n in range(4)], axis=1)

    def unfolded(value):
        return jnp.concatenate([value[:, n * COLS : (n + 1) * COLS] for n in range(4)], axis=0)

    def shot_send(value):
        value = jnp.concatenate([folded(value), jnp.zeros((COLS // 2, TB - 4 * COLS), F32)], axis=1)
        shot_msg[...] = value
        shot[r] = value
        for n in range(1, N_ROW):
            pltpu.make_async_remote_copy(
                src_ref=shot_msg,
                dst_ref=shot.at[r],
                send_sem=fs_sem.at[3],
                recv_sem=fr_sem.at[3],
                device_id=(g, lax.rem(r + n, N_ROW)),
                device_id_type=MESH,
            ).start()
        for step, target in far_edges:
            pltpu.make_async_remote_copy(
                src_ref=shot_msg,
                dst_ref=shot.at[N_ROW + r],
                send_sem=as_sem.at[1],
                recv_sem=ar_sem.at[1],
                device_id=(lax.rem(g + step, N_GRP), target),
                device_id_type=MESH,
            ).start()

    def shot_sum():
        wait_bytes(shot.at[pl.ds(0, N_ROW - 1)], fr_sem.at[3])

        @pl.when(border)
        def _():
            wait_bytes(shot.at[pl.ds(0, N_ROW)], ar_sem.at[1])

        sums = []
        for at in (0, N_ROW):
            terms = [shot[at + n] for n in range(N_ROW)]
            while len(terms) > 1:
                terms = [terms[n] + terms[n + 1] for n in range(0, len(terms), 2)]
            sums.append(terms[0])
        return unfolded(jnp.where(lost_of[0], sums[1], sums[0]))

    def prepare(w, ref, at):
        for p in range(2 * REACH + 1):
            group = lax.rem(d + (p - REACH) + total_devices, total_devices) // N_ROW
            own = jnp.where(group == g, 1.0, 0.0).astype(BF16)
            for q in range(BR):
                hi, lo = split(win[w, p * BR + q])
                hi_own = hi * own
                lo_own = lo * own
                ref[p * BR + q, at : at + 4 * COLS] = jnp.concatenate(
                    [hi_own, lo_own, hi - hi_own, lo - lo_own], axis=0
                )

    def product(ref, count):
        own = [[] for _ in range(count)]
        other = [[] for _ in range(count)]
        rows = 4 * COLS * count
        for i in range(BR):
            for k in range(K):
                rhs[i, 0:rows, k * TB : (k + 1) * TB] = ref[local[i, k]]
            o = lax.dot_general(hl[i], rhs[i, 0:rows], (((1,), (1,)), ((), ())), preferred_element_type=F32)
            o = (o[:TB] + o[TB:]).T
            for n in range(count):
                own[n].append(o[4 * n * COLS : (4 * n + 1) * COLS] + o[(4 * n + 1) * COLS : (4 * n + 2) * COLS])
                other[n].append(
                    o[(4 * n + 2) * COLS : (4 * n + 3) * COLS] + o[(4 * n + 3) * COLS : (4 * n + 4) * COLS]
                )
        return [jnp.concatenate(v, axis=1) for v in own], [jnp.concatenate(v, axis=1) for v in other]

    def condition(*vectors):
        out = [[] for _ in vectors]
        for i in range(BR):
            parts = []
            for v in vectors:
                parts.extend(split(v[:, i * TB : (i + 1) * TB]))
            o = lax.dot_general(
                zhl[i], jnp.concatenate(parts, axis=0), (((1,), (1,)), ((), ())), preferred_element_type=F32
            )
            o = (o[:TB] + o[TB:]).T
            for n in range(len(vectors)):
                out[n].append(o[2 * n * COLS : (2 * n + 1) * COLS] + o[(2 * n + 1) * COLS : (2 * n + 2) * COLS])
        return [jnp.concatenate(v, axis=1) for v in out]

    def put(w, v):
        for i in range(BR):
            win[w, BAND + i] = v[:, i * TB : (i + 1) * TB]

    def lanes(m, *spans):
        return jnp.concatenate([m[a : a + COLS, b : b + n] for a, b, n in spans], axis=1)

    def stack(*parts):
        return jnp.concatenate(parts, axis=0)

    loads[0].wait()
    pl.semaphore_wait(barrier, len(offsets) + CELL - 1 + FAR - 1)
    halo_send(WB)
    loads[1].wait()
    for i in range(BR):
        hi, lo = split(zstage[i])
        zhl[i, 0:TB] = hi
        zhl[i, TB : 2 * TB] = lo
    v0 = jnp.concatenate([win[WB, BAND + i] for i in range(BR)], axis=1)
    (zb,) = condition(v0)
    put(WZ, zb)
    halo_send(WZ)
    for n in range(CELLS):
        side[CELLS + n] = jnp.zeros((COLS, TB), F32)
    for n in range(N_ROW):
        shot[N_ROW + n] = jnp.zeros((COLS // 2, TB), F32)

    loads[2].wait()

    def localise(k, carry):
        for i in range(BR):
            local[i, k] = jnp.clip(cols_ref[i, k] - first, 0, WIN - 1)
        return carry

    lax.fori_loop(0, K, localise, 0)
    for i in range(BR):
        loads[4 + i].wait()

        def convert(k, carry, i=i):
            hi, lo = split(stage[i, k])
            at = pl.ds(pl.multiple_of(k * TB, TB), TB)
            hl[i, 0:TB, at] = hi
            hl[i, TB : 2 * TB, at] = lo
            return carry

        lax.fori_loop(0, K, convert, 0)
    halo_wait(WB)
    prepare(WB, winb, 0)
    (own,), (p0,) = product(winb, 1)
    v1 = own + p0 - v0
    put(WV, v1)
    halo_send(WV)
    (zp0,) = condition(p0)
    put(WP, zp0)
    halo_send(WP)
    basis = stack(v0, v1)
    ga = mm(basis, basis, 1, 1)
    near_send(0, lanes(ga, (0, 0, 32), (16, 0, 32)))
    loads[3].wait()
    lost = lax.rem(lost_ref[0], N_GRP)
    touch = jnp.logical_and(border, jnp.where(r < N_ROW // 2, g - 1, g + 1) == lost)
    is_lost = g == lost
    lost_of[0] = touch
    halo_wait(WZ)
    prepare(WZ, winc, 0)
    far_send(0)
    halo_wait(WV)
    prepare(WV, winb, 0)
    (own,), (p1,) = product(winb, 1)
    v2 = own + p1 - v1
    near_send(1, folded(mm(basis, v2, 1, 1)))
    (zp1,) = condition(p1)
    put(WQ, zp1)
    halo_send(WQ)
    one = eye16()
    ga = far_all(0)
    ga = stack(ga[:, 0:32], ga[:, 32:64])
    g00 = sym(ga[0:16, 0:16])
    half = sym(ga[0:16, 16:32])
    e0, inv0 = eliminate((g00 + half, half), (g00, one))
    a0 = one - e0
    c = stack(e0, -a0)
    squares = mm(c, mm(ga, c), 0, 0)
    far_send(1)
    m0 = mm(inv0, squares)
    d0 = e0 + m0
    d1 = -a0
    dd = stack(d0, d1)
    curve = mm(dd, mm(ga, stack(d0, d0 + d1)), 0, 0)
    halo_wait(WP)
    prepare(WP, winc, 4 * COLS)
    halo_wait(WQ)
    prepare(WQ, winc, 8 * COLS)
    (bz, bzp0, bzp1), (oz, ozp0, ozp1) = product(winc, 3)
    y, yp0, yp1 = condition(bz, bzp0, bzp1)
    gb = unfolded(far_all(1))
    curve = curve + mm(dd, mm(gb, d1), 0, 0)
    (a1,) = eliminate((sym(curve), squares))
    cs = mm(dd, a1) + stack(a0, jnp.zeros_like(a0))
    t0 = y - mm(cs, stack(yp0, yp1), 0, 0)
    put(WT, t0)
    halo_send(WT)
    coupled = mm(cs, stack(p0, p1), 0, 0)
    rr = v0 - coupled
    s0 = zb - mm(cs, stack(zp0, zp1), 0, 0)
    q0 = bz - mm(cs, stack(bzp0, bzp1), 0, 0)
    g2 = mm(stack(rr, s0, q0), stack(s0, q0, t0), 1, 1)
    near_send(2, lanes(g2, (0, 0, 16), (0, 32, 16), (16, 16, 16), (32, 32, 16)))
    ps0 = oz - mm(cs, stack(ozp0, ozp1), 0, 0)
    base_rec = mm(cs, basis, 0, 0)
    d0a = mm(d0, a1)
    d1a = mm(d1, a1)
    rc = stack(e0 - d0a, -(a0 + d0a + d1a), -d1a)
    residual = mm(rc, stack(v0, v1, v2), 0, 0)
    st = stack(s0, t0)
    side_send(2)
    halo_wait(WT)
    prepare(WT, winb, 0)
    (q1,), (ps1,) = product(winb, 1)
    g3 = mm(st, q1, 1, 1)
    shot_send(g3)
    g2 = side_sum(2)
    w0 = g2[:, 0:16]
    rt, sq, qt = g2[:, 16:32], g2[:, 32:48], g2[:, 48:64]
    b0, invw = eliminate((sym(sq), w0), (sym(w0), one))
    w1 = w0 - mm(rt, b0) + mm(b0, mm(qt, b0) - sq.T, 0, 0)
    n0 = one + mm(invw, w1)
    nb = stack(n0, -b0)
    bend = mm(nb, mm(stack(sq, qt.T), n0), 0, 0)
    base = jnp.where(is_lost, rr, residual + jnp.where(touch, coupled, 0.0))
    xs = stack(jnp.where(is_lost, q0, ps0), jnp.where(is_lost, q1, ps1))
    g3 = shot_sum()
    bend = bend - mm(nb, mm(g3, b0), 0, 0)
    (b1,) = eliminate((sym(bend), w1))
    es = mm(nb, b1) + stack(b0, jnp.zeros_like(b0))
    rec = jnp.where(is_lost, mm(es, st, 0, 0), base_rec)
    tres = jnp.where(jnp.logical_or(is_lost, touch), base - mm(es, xs, 0, 0), base)
    for i in range(BR):
        rec_ref[i] = rec[:, i * TB : (i + 1) * TB]
        tres_ref[i] = tres[:, i * TB : (i + 1) * TB]
    for w in range(WINS):
        wait_bytes(win.at[w, pl.ds(0, WIN - BR)], hs_sem.at[w])
    for gm in range(3):
        wait_bytes(nears[gm].at[pl.ds(0, CELL - 1)], ns_sem.at[gm])
    for gm in range(2):
        wait_bytes(fars[gm].at[pl.ds(0, FAR - 1)], fs_sem.at[gm])
    wait_bytes(side.at[pl.ds(0, CELLS - 1)], fs_sem.at[2])
    wait_bytes(side.at[pl.ds(0, 2)], as_sem.at[0])
    wait_bytes(shot.at[pl.ds(0, N_ROW - 1)], fs_sem.at[3])
    wait_bytes(shot.at[pl.ds(0, len(far_edges))], as_sem.at[1])


def per_device(matrix_tiles, column_index, precond, right_side, lost_group):
    vmem = pl.BlockSpec(memory_space=pltpu.VMEM)
    hbm = pl.BlockSpec(memory_space=pltpu.HBM)
    shape = jax.ShapeDtypeStruct((BR, COLS, TB), F32)
    dma = pltpu.SemaphoreType.DMA
    return pl.pallas_call(
        kernel,
        out_shape=(shape, shape),
        in_specs=[hbm, hbm, hbm, hbm, hbm],
        out_specs=(vmem, vmem),
        scratch_shapes=[
            pltpu.VMEM((BR, K, TB, TB), F32),
            pltpu.VMEM((BR, TB, TB), F32),
            pltpu.VMEM((BR, 2 * TB, K * TB), BF16),
            pltpu.VMEM((BR, 2 * TB, TB), BF16),
            pltpu.VMEM((WINS, WIN, COLS, TB), F32),
            pltpu.VMEM((WIN, 4 * COLS, TB), BF16),
            pltpu.VMEM((WIN, 12 * COLS, TB), BF16),
            pltpu.VMEM((BR, 12 * COLS, K * TB), BF16),
            pltpu.VMEM((2, COLS, TB), F32),
            pltpu.VMEM((2, COLS // 2, TB), F32),
            pltpu.VMEM((2, COLS, TB), F32),
            pltpu.VMEM((CELL, COLS, TB), F32),
            pltpu.VMEM((CELL, COLS // 2, TB), F32),
            pltpu.VMEM((CELL, COLS, TB), F32),
            pltpu.VMEM((FAR, COLS, TB), F32),
            pltpu.VMEM((FAR, COLS // 2, TB), F32),
            pltpu.VMEM((2 * CELLS, COLS, TB), F32),
            pltpu.VMEM((2 * N_ROW, COLS // 2, TB), F32),
            pltpu.VMEM((COLS // 2, TB), F32),
            pltpu.SMEM((BR, K), jnp.int32),
            pltpu.SMEM((1,), jnp.int32),
            pltpu.SMEM((BR, K), jnp.int32),
            dma((4 + BR,)),
            dma((WINS,)),
            dma((WINS,)),
            dma((3,)),
            dma((3,)),
            dma((4,)),
            dma((4,)),
            dma((2,)),
            dma((2,)),
        ],
        compiler_params=pltpu.CompilerParams(
            collective_id=0, has_side_effects=True, vmem_limit_bytes=55136 * 1024
        ),
        name="recover",
    )(column_index, lost_group, matrix_tiles, precond, right_side)


def solution(mesh):
    in_specs = (
        P(("grp", "row"), None, None, None),
        P(("grp", "row"), None),
        P(("grp", "row"), None, None),
        P(("grp", "row"), None, None),
        P(),
    )
    out_specs = (P(("grp", "row"), None, None), P(("grp", "row"), None, None))
    return jax.shard_map(
        per_device, mesh=mesh, in_specs=in_specs, out_specs=out_specs, check_vma=False
    )
```

```python
import functools

import jax
import jax.numpy as jnp
from jax import lax
from jax.experimental import pallas as pl
from jax.experimental.pallas import tpu as pltpu
from jax.sharding import PartitionSpec as P

BAND = 12
F32 = jnp.float32
BF16 = jnp.bfloat16
MESH = pl.DeviceIdType.MESH
N_GRP, N_ROW, BR, K, COLS, TB = 4, 32, 4, 32, 16, 128
REACH = 3
WIN = BR * (2 * REACH + 1)
CELL = 8
FAR = (N_GRP * N_ROW) // CELL
CELLS = N_ROW // CELL
WB, WZ, WV, WP, WQ, WT = range(6)
WINS = 6


def farthest_first(steps):
    def hops(step):
        return -sum(min(n, size - n) * weight for n, size, weight in zip(step, *steps[1:]))

    return sorted(steps[0], key=hops)


NEAR_STEPS = farthest_first(([(z, c) for z in range(4) for c in range(2) if z + c], (4, 2), (2, 1)))
FAR_STEPS = farthest_first(([(x, y) for x in range(4) for y in range(4) if x + y], (4, 4), (1, 1)))
SHOT_STEPS = farthest_first(
    ([(y, z, c) for y in range(4) for z in range(4) for c in range(2) if y + z + c], (4, 4, 2), (2, 2, 1))
)


def mm(a, b, ca=1, cb=0):
    return lax.dot_general(
        a, b, (((ca,), (cb,)), ((), ())), precision=lax.Precision.HIGHEST, preferred_element_type=F32
    )


def split(x):
    hi = x.astype(BF16)
    return hi, (x - hi.astype(F32)).astype(BF16)


def eye16():
    r = lax.broadcasted_iota(jnp.int32, (COLS, COLS), 0)
    c = lax.broadcasted_iota(jnp.int32, (COLS, COLS), 1)
    return (r == c).astype(F32)


def sym(g):
    return 0.5 * (g + g.T)


def eliminate(*systems):
    mats = [jnp.concatenate([s, h], axis=1) for s, h in systems]
    shape = mats[0].shape
    rows = lax.broadcasted_iota(jnp.int32, shape, 0)
    columns = [[jnp.broadcast_to(m[:, j : j + 1], shape) for j in range(COLS)] for m in mats]

    def step(value, column, inverse, j):
        row = value[j : j + 1] * inverse
        return jnp.where(rows == j, row, value - column * row)

    for j in range(COLS):
        for n in range(len(mats)):
            column = columns[n][j]
            inverse = 1.0 / column[j : j + 1]
            mats[n] = step(mats[n], column, inverse, j)
            for u in range(j + 1, COLS):
                columns[n][u] = step(columns[n][u], column, inverse, j)
    return [m[:, COLS:] for m in mats]


def kernel(
    cols_hbm, lost_hbm, tiles_ref, pre_hbm, b_hbm, rec_ref, tres_ref,
    stage, zstage, hl, zhl, win, winb, winc, rhs, msg0, msg1, msg2, near0, near1, near2, far0, far1, side, shot, shot_msg, cols_ref, lost_ref, local,
    load_sem, hs_sem, hr_sem, ns_sem, nr_sem, fs_sem, fr_sem, as_sem, ar_sem,
):
    g = lax.axis_index("grp")
    r = lax.axis_index("row")
    d = g * N_ROW + r
    cell = r // CELL
    pos = lax.rem(r, CELL)
    my_far = g * CELLS + cell
    first = d * BR - BAND
    total_devices = N_GRP * N_ROW

    def place(step_z, step_c):
        return lax.rem(pos // 2 + step_z, CELL // 2) * 2 + lax.rem(pos + step_c, 2)

    def near_dev(step):
        return (g, cell * CELL + place(*step))

    def far_dev(step):
        return (lax.rem(g + step[0], N_GRP), lax.rem(cell + step[1], CELLS) * CELL + pos)

    def shot_dev(step):
        return (g, lax.rem(cell + step[0], CELLS) * CELL + place(*step[1:]))

    def halo_dev(o):
        t = lax.rem(d + o + total_devices, total_devices)
        return (t // N_ROW, lax.rem(t, N_ROW))

    border = jnp.logical_or(r < REACH, r >= N_ROW - REACH)
    offsets = [3, -3, 2, -2, 1, -1]
    fars = [far0, far1]
    nears = [near0, near1, near2]
    msgs = [msg0, msg1, msg2]

    barrier = pltpu.get_barrier_semaphore()
    for o in offsets:
        pl.semaphore_signal(barrier, inc=1, device_id=halo_dev(o), device_id_type=MESH)
    for n in FAR_STEPS:
        pl.semaphore_signal(barrier, inc=1, device_id=far_dev(n), device_id_type=MESH)
    for n in NEAR_STEPS:
        pl.semaphore_signal(barrier, inc=1, device_id=near_dev(n), device_id_type=MESH)

    own_span = pl.ds(BAND, BR)
    loads = [
        pltpu.make_async_copy(b_hbm, win.at[WB, own_span], load_sem.at[0]),
        pltpu.make_async_copy(pre_hbm, zstage, load_sem.at[1]),
        pltpu.make_async_copy(cols_hbm, cols_ref, load_sem.at[2]),
        pltpu.make_async_copy(lost_hbm, lost_ref, load_sem.at[3]),
    ] + [pltpu.make_async_copy(tiles_ref.at[i], stage.at[i], load_sem.at[4 + i]) for i in range(BR)]
    for load in loads:
        load.start()

    def wait_bytes(ref, sem):
        pltpu.make_async_copy(ref, ref, sem).wait()

    def halo_send(w):
        for o in offsets:
            pltpu.make_async_remote_copy(
                src_ref=win.at[w, own_span],
                dst_ref=win.at[w, pl.ds((REACH - o) * BR, BR)],
                send_sem=hs_sem.at[w],
                recv_sem=hr_sem.at[w],
                device_id=halo_dev(o),
                device_id_type=MESH,
            ).start()

    def halo_wait(w):
        wait_bytes(win.at[w, pl.ds(0, WIN - BR)], hr_sem.at[w])

    def near_send(gm, value):
        msg, near = msgs[gm], nears[gm]
        n_lanes = value.shape[1]
        value = jnp.concatenate([value, jnp.zeros((value.shape[0], TB - n_lanes), F32)], axis=1)
        msg[0] = value
        near[pos] = value
        for n in NEAR_STEPS:
            pltpu.make_async_remote_copy(
                src_ref=msg.at[0],
                dst_ref=near.at[pos],
                send_sem=ns_sem.at[gm],
                recv_sem=nr_sem.at[gm],
                device_id=near_dev(n),
                device_id_type=MESH,
            ).start()

    def near_sum(gm):
        msg, near = msgs[gm], nears[gm]
        wait_bytes(near.at[pl.ds(0, CELL - 1)], nr_sem.at[gm])
        terms = [near[n] for n in range(CELL)]
        while len(terms) > 1:
            terms = [terms[n] + terms[n + 1] for n in range(0, len(terms), 2)]
        msg[1] = terms[0]
        return terms[0]

    def far_send(gm):
        far = fars[gm]
        far[my_far] = near_sum(gm)
        for n in FAR_STEPS:
            pltpu.make_async_remote_copy(
                src_ref=msgs[gm].at[1],
                dst_ref=far.at[my_far],
                send_sem=fs_sem.at[gm],
                recv_sem=fr_sem.at[gm],
                device_id=far_dev(n),
                device_id_type=MESH,
            ).start()

    def far_all(gm):
        far = fars[gm]
        wait_bytes(far.at[pl.ds(0, FAR - 1)], fr_sem.at[gm])
        terms = [far[n] for n in range(FAR)]
        while len(terms) > 1:
            terms = [terms[n] + terms[n + 1] for n in range(0, len(terms), 2)]
        return terms[0]

    def side_send(gm):
        side[cell] = near_sum(gm)
        for n in (2, 1, 3):
            pltpu.make_async_remote_copy(
                src_ref=msgs[gm].at[1],
                dst_ref=side.at[cell],
                send_sem=fs_sem.at[gm],
                recv_sem=fr_sem.at[gm],
                device_id=(g, lax.rem(cell + n, CELLS) * CELL + pos),
                device_id_type=MESH,
            ).start()
        for step, target in ((1, 0), (N_GRP - 1, CELLS - 1)):
            pltpu.make_async_remote_copy(
                src_ref=msgs[gm].at[1],
                dst_ref=side.at[CELLS + cell],
                send_sem=as_sem.at[0],
                recv_sem=ar_sem.at[0],
                device_id=(lax.rem(g + step, N_GRP), target * CELL + pos),
                device_id_type=MESH,
            ).start()

    lost_of = [None]

    def side_sum(gm):
        wait_bytes(side.at[pl.ds(0, CELLS - 1)], fr_sem.at[gm])

        @pl.when(jnp.logical_or(cell == 0, cell == CELLS - 1))
        def _():
            wait_bytes(side.at[pl.ds(0, CELLS)], ar_sem.at[0])

        own = (side[0] + side[1]) + (side[2] + side[3])
        other = (side[4] + side[5]) + (side[6] + side[7])
        return jnp.where(lost_of[0], other, own)

    far_edges = [(1, 0), (1, 1), (1, 2), (N_GRP - 1, N_ROW - 1), (N_GRP - 1, N_ROW - 2), (N_GRP - 1, N_ROW - 3)]

    def folded(value):
        half = COLS // 2
        return jnp.concatenate([value[n * half : (n + 1) * half] for n in range(4)], axis=1)

    def unfolded(value):
        return jnp.concatenate([value[:, n * COLS : (n + 1) * COLS] for n in range(4)], axis=0)

    def shot_send(value):
        value = jnp.concatenate([folded(value), jnp.zeros((COLS // 2, TB - 4 * COLS), F32)], axis=1)
        shot_msg[...] = value
        shot[r] = value
        for step, target in far_edges:
            pltpu.make_async_remote_copy(
                src_ref=shot_msg,
                dst_ref=shot.at[N_ROW + r],
                send_sem=as_sem.at[1],
                recv_sem=ar_sem.at[1],
                device_id=(lax.rem(g + step, N_GRP), target),
                device_id_type=MESH,
            ).start()
        for n in SHOT_STEPS:
            pltpu.make_async_remote_copy(
                src_ref=shot_msg,
                dst_ref=shot.at[r],
                send_sem=fs_sem.at[3],
                recv_sem=fr_sem.at[3],
                device_id=shot_dev(n),
                device_id_type=MESH,
            ).start()

    def shot_sum():
        wait_bytes(shot.at[pl.ds(0, N_ROW - 1)], fr_sem.at[3])

        @pl.when(border)
        def _():
            wait_bytes(shot.at[pl.ds(0, N_ROW)], ar_sem.at[1])

        sums = []
        for at in (0, N_ROW):
            terms = [shot[at + n] for n in range(N_ROW)]
            while len(terms) > 1:
                terms = [terms[n] + terms[n + 1] for n in range(0, len(terms), 2)]
            sums.append(terms[0])
        return unfolded(jnp.where(lost_of[0], sums[1], sums[0]))

    def prepare(w, ref, at):
        for p in range(2 * REACH + 1):
            group = lax.rem(d + (p - REACH) + total_devices, total_devices) // N_ROW
            own = jnp.where(group == g, 1.0, 0.0).astype(BF16)
            for q in range(BR):
                hi, lo = split(win[w, p * BR + q])
                hi_own = hi * own
                lo_own = lo * own
                ref[p * BR + q, at : at + 4 * COLS] = jnp.concatenate(
                    [hi_own, lo_own, hi - hi_own, lo - lo_own], axis=0
                )

    def product(ref, count):
        own = [[] for _ in range(count)]
        other = [[] for _ in range(count)]
        rows = 4 * COLS * count
        for i in range(BR):
            for k in range(K):
                rhs[i, 0:rows, k * TB : (k + 1) * TB] = ref[local[i, k]]
            o = lax.dot_general(hl[i], rhs[i, 0:rows], (((1,), (1,)), ((), ())), preferred_element_type=F32)
            o = (o[:TB] + o[TB:]).T
            for n in range(count):
                own[n].append(o[4 * n * COLS : (4 * n + 1) * COLS] + o[(4 * n + 1) * COLS : (4 * n + 2) * COLS])
                other[n].append(
                    o[(4 * n + 2) * COLS : (4 * n + 3) * COLS] + o[(4 * n + 3) * COLS : (4 * n + 4) * COLS]
                )
        return [jnp.concatenate(v, axis=1) for v in own], [jnp.concatenate(v, axis=1) for v in other]

    def condition(*vectors):
        out = [[] for _ in vectors]
        for i in range(BR):
            parts = []
            for v in vectors:
                parts.extend(split(v[:, i * TB : (i + 1) * TB]))
            o = lax.dot_general(
                zhl[i], jnp.concatenate(parts, axis=0), (((1,), (1,)), ((), ())), preferred_element_type=F32
            )
            o = (o[:TB] + o[TB:]).T
            for n in range(len(vectors)):
                out[n].append(o[2 * n * COLS : (2 * n + 1) * COLS] + o[(2 * n + 1) * COLS : (2 * n + 2) * COLS])
        return [jnp.concatenate(v, axis=1) for v in out]

    def put(w, v):
        for i in range(BR):
            win[w, BAND + i] = v[:, i * TB : (i + 1) * TB]

    def lanes(m, *spans):
        return jnp.concatenate([m[a : a + COLS, b : b + n] for a, b, n in spans], axis=1)

    def stack(*parts):
        return jnp.concatenate(parts, axis=0)

    loads[0].wait()
    pl.semaphore_wait(barrier, len(offsets) + CELL - 1 + FAR - 1)
    halo_send(WB)
    loads[1].wait()
    for i in range(BR):
        hi, lo = split(zstage[i])
        zhl[i, 0:TB] = hi
        zhl[i, TB : 2 * TB] = lo
    v0 = jnp.concatenate([win[WB, BAND + i] for i in range(BR)], axis=1)
    (zb,) = condition(v0)
    put(WZ, zb)
    halo_send(WZ)
    for n in range(CELLS):
        side[CELLS + n] = jnp.zeros((COLS, TB), F32)
    for n in range(N_ROW):
        shot[N_ROW + n] = jnp.zeros((COLS // 2, TB), F32)

    loads[2].wait()

    def localise(k, carry):
        for i in range(BR):
            local[i, k] = jnp.clip(cols_ref[i, k] - first, 0, WIN - 1)
        return carry

    lax.fori_loop(0, K, localise, 0)
    for i in range(BR):
        loads[4 + i].wait()

        def convert(k, carry, i=i):
            hi, lo = split(stage[i, k])
            at = pl.ds(pl.multiple_of(k * TB, TB), TB)
            hl[i, 0:TB, at] = hi
            hl[i, TB : 2 * TB, at] = lo
            return carry

        lax.fori_loop(0, K, convert, 0)
    halo_wait(WB)
    prepare(WB, winb, 0)
    (own,), (p0,) = product(winb, 1)
    v1 = own + p0 - v0
    put(WV, v1)
    halo_send(WV)
    (zp0,) = condition(p0)
    put(WP, zp0)
    halo_send(WP)
    basis = stack(v0, v1)
    ga = mm(basis, basis, 1, 1)
    near_send(0, lanes(ga, (0, 0, 32), (16, 0, 32)))
    loads[3].wait()
    lost = lax.rem(lost_ref[0], N_GRP)
    touch = jnp.logical_and(border, jnp.where(r < N_ROW // 2, g - 1, g + 1) == lost)
    is_lost = g == lost
    lost_of[0] = touch
    halo_wait(WZ)
    prepare(WZ, winc, 0)
    far_send(0)
    halo_wait(WV)
    prepare(WV, winb, 0)
    (own,), (p1,) = product(winb, 1)
    v2 = own + p1 - v1
    near_send(1, folded(mm(basis, v2, 1, 1)))
    (zp1,) = condition(p1)
    put(WQ, zp1)
    halo_send(WQ)
    one = eye16()
    ga = far_all(0)
    ga = stack(ga[:, 0:32], ga[:, 32:64])
    g00 = sym(ga[0:16, 0:16])
    half = sym(ga[0:16, 16:32])
    e0, inv0 = eliminate((g00 + half, half), (g00, one))
    a0 = one - e0
    c = stack(e0, -a0)
    squares = mm(c, mm(ga, c), 0, 0)
    far_send(1)
    m0 = mm(inv0, squares)
    d0 = e0 + m0
    d1 = -a0
    dd = stack(d0, d1)
    curve = mm(dd, mm(ga, stack(d0, d0 + d1)), 0, 0)
    halo_wait(WP)
    prepare(WP, winc, 4 * COLS)
    halo_wait(WQ)
    prepare(WQ, winc, 8 * COLS)
    (bz, bzp0, bzp1), (oz, ozp0, ozp1) = product(winc, 3)
    y, yp0, yp1 = condition(bz, bzp0, bzp1)
    gb = unfolded(far_all(1))
    curve = curve + mm(dd, mm(gb, d1), 0, 0)
    (a1,) = eliminate((sym(curve), squares))
    cs = mm(dd, a1) + stack(a0, jnp.zeros_like(a0))
    t0 = y - mm(cs, stack(yp0, yp1), 0, 0)
    put(WT, t0)
    halo_send(WT)
    coupled = mm(cs, stack(p0, p1), 0, 0)
    rr = v0 - coupled
    s0 = zb - mm(cs, stack(zp0, zp1), 0, 0)
    q0 = bz - mm(cs, stack(bzp0, bzp1), 0, 0)
    g2 = mm(stack(rr, s0, q0), stack(s0, q0, t0), 1, 1)
    near_send(2, lanes(g2, (0, 0, 16), (0, 32, 16), (16, 16, 16), (32, 32, 16)))
    ps0 = oz - mm(cs, stack(ozp0, ozp1), 0, 0)
    base_rec = mm(cs, basis, 0, 0)
    d0a = mm(d0, a1)
    d1a = mm(d1, a1)
    rc = stack(e0 - d0a, -(a0 + d0a + d1a), -d1a)
    residual = mm(rc, stack(v0, v1, v2), 0, 0)
    st = stack(s0, t0)
    side_send(2)
    halo_wait(WT)
    prepare(WT, winb, 0)
    (q1,), (ps1,) = product(winb, 1)
    g3 = mm(st, q1, 1, 1)
    shot_send(g3)
    g2 = side_sum(2)
    w0 = g2[:, 0:16]
    rt, sq, qt = g2[:, 16:32], g2[:, 32:48], g2[:, 48:64]
    b0, invw = eliminate((sym(sq), w0), (sym(w0), one))
    w1 = w0 - mm(rt, b0) + mm(b0, mm(qt, b0) - sq.T, 0, 0)
    n0 = one + mm(invw, w1)
    nb = stack(n0, -b0)
    bend = mm(nb, mm(stack(sq, qt.T), n0), 0, 0)
    base = jnp.where(is_lost, rr, residual + jnp.where(touch, coupled, 0.0))
    xs = stack(jnp.where(is_lost, q0, ps0), jnp.where(is_lost, q1, ps1))
    g3 = shot_sum()
    bend = bend - mm(nb, mm(g3, b0), 0, 0)
    (b1,) = eliminate((sym(bend), w1))
    es = mm(nb, b1) + stack(b0, jnp.zeros_like(b0))
    rec = jnp.where(is_lost, mm(es, st, 0, 0), base_rec)
    tres = jnp.where(jnp.logical_or(is_lost, touch), base - mm(es, xs, 0, 0), base)
    for i in range(BR):
        rec_ref[i] = rec[:, i * TB : (i + 1) * TB]
        tres_ref[i] = tres[:, i * TB : (i + 1) * TB]
    for w in range(WINS):
        wait_bytes(win.at[w, pl.ds(0, WIN - BR)], hs_sem.at[w])
    for gm in range(3):
        wait_bytes(nears[gm].at[pl.ds(0, CELL - 1)], ns_sem.at[gm])
    for gm in range(2):
        wait_bytes(fars[gm].at[pl.ds(0, FAR - 1)], fs_sem.at[gm])
    wait_bytes(side.at[pl.ds(0, CELLS - 1)], fs_sem.at[2])
    wait_bytes(side.at[pl.ds(0, 2)], as_sem.at[0])
    wait_bytes(shot.at[pl.ds(0, N_ROW - 1)], fs_sem.at[3])
    wait_bytes(shot.at[pl.ds(0, len(far_edges))], as_sem.at[1])


def per_device(matrix_tiles, column_index, precond, right_side, lost_group):
    vmem = pl.BlockSpec(memory_space=pltpu.VMEM)
    hbm = pl.BlockSpec(memory_space=pltpu.HBM)
    shape = jax.ShapeDtypeStruct((BR, COLS, TB), F32)
    dma = pltpu.SemaphoreType.DMA
    return pl.pallas_call(
        kernel,
        out_shape=(shape, shape),
        in_specs=[hbm, hbm, hbm, hbm, hbm],
        out_specs=(vmem, vmem),
        scratch_shapes=[
            pltpu.VMEM((BR, K, TB, TB), F32),
            pltpu.VMEM((BR, TB, TB), F32),
            pltpu.VMEM((BR, 2 * TB, K * TB), BF16),
            pltpu.VMEM((BR, 2 * TB, TB), BF16),
            pltpu.VMEM((WINS, WIN, COLS, TB), F32),
            pltpu.VMEM((WIN, 4 * COLS, TB), BF16),
            pltpu.VMEM((WIN, 12 * COLS, TB), BF16),
            pltpu.VMEM((BR, 12 * COLS, K * TB), BF16),
            pltpu.VMEM((2, COLS, TB), F32),
            pltpu.VMEM((2, COLS // 2, TB), F32),
            pltpu.VMEM((2, COLS, TB), F32),
            pltpu.VMEM((CELL, COLS, TB), F32),
            pltpu.VMEM((CELL, COLS // 2, TB), F32),
            pltpu.VMEM((CELL, COLS, TB), F32),
            pltpu.VMEM((FAR, COLS, TB), F32),
            pltpu.VMEM((FAR, COLS // 2, TB), F32),
            pltpu.VMEM((2 * CELLS, COLS, TB), F32),
            pltpu.VMEM((2 * N_ROW, COLS // 2, TB), F32),
            pltpu.VMEM((COLS // 2, TB), F32),
            pltpu.SMEM((BR, K), jnp.int32),
            pltpu.SMEM((1,), jnp.int32),
            pltpu.SMEM((BR, K), jnp.int32),
            dma((4 + BR,)),
            dma((WINS,)),
            dma((WINS,)),
            dma((3,)),
            dma((3,)),
            dma((4,)),
            dma((4,)),
            dma((2,)),
            dma((2,)),
        ],
        compiler_params=pltpu.CompilerParams(
            collective_id=0, has_side_effects=True, vmem_limit_bytes=55136 * 1024
        ),
        name="recover",
    )(column_index, lost_group, matrix_tiles, precond, right_side)


def solution(mesh):
    in_specs = (
        P(("grp", "row"), None, None, None),
        P(("grp", "row"), None),
        P(("grp", "row"), None, None),
        P(("grp", "row"), None, None),
        P(),
    )
    out_specs = (P(("grp", "row"), None, None), P(("grp", "row"), None, None))
    return jax.shard_map(
        per_device, mesh=mesh, in_specs=in_specs, out_specs=out_specs, check_vma=False
    )
```

```python
import functools

import jax
import jax.numpy as jnp
from jax import lax
from jax.experimental import pallas as pl
from jax.experimental.pallas import tpu as pltpu
from jax.sharding import PartitionSpec as P

BAND = 12
F32 = jnp.float32
BF16 = jnp.bfloat16
MESH = pl.DeviceIdType.MESH
N_GRP, N_ROW, BR, K, COLS, TB = 4, 32, 4, 32, 16, 128
REACH = 3
WIN = BR * (2 * REACH + 1)
CELL = 8
FAR = (N_GRP * N_ROW) // CELL
CELLS = N_ROW // CELL
WB, WZ, WV, WP, WQ, WT = range(6)
WINS = 6


def farthest_first(steps):
    def hops(step):
        return -sum(min(n, size - n) * weight for n, size, weight in zip(step, *steps[1:]))

    return sorted(steps[0], key=hops)


NEAR_STEPS = farthest_first(([(z, c) for z in range(4) for c in range(2) if z + c], (4, 2), (2, 1)))
FAR_STEPS = farthest_first(([(x, y) for x in range(4) for y in range(4) if x + y], (4, 4), (1, 1)))
SHOT_STEPS = farthest_first(
    ([(y, z, c) for y in range(4) for z in range(4) for c in range(2) if y + z + c], (4, 4, 2), (2, 2, 1))
)


def mm(a, b, ca=1, cb=0):
    return lax.dot_general(
        a, b, (((ca,), (cb,)), ((), ())), precision=lax.Precision.HIGHEST, preferred_element_type=F32
    )


def split(x):
    hi = x.astype(BF16)
    return hi, (x - hi.astype(F32)).astype(BF16)


def eye16():
    r = lax.broadcasted_iota(jnp.int32, (COLS, COLS), 0)
    c = lax.broadcasted_iota(jnp.int32, (COLS, COLS), 1)
    return (r == c).astype(F32)


def sym(g):
    return 0.5 * (g + g.T)


def eliminate(*systems):
    mats = [jnp.concatenate([s, h], axis=1) for s, h in systems]
    shape = mats[0].shape
    rows = lax.broadcasted_iota(jnp.int32, shape, 0)
    columns = [[jnp.broadcast_to(m[:, j : j + 1], shape) for j in range(COLS)] for m in mats]

    def step(value, column, inverse, j):
        row = value[j : j + 1] * inverse
        return jnp.where(rows == j, row, value - column * row)

    for j in range(COLS):
        for n in range(len(mats)):
            column = columns[n][j]
            inverse = 1.0 / column[j : j + 1]
            mats[n] = step(mats[n], column, inverse, j)
            for u in range(j + 1, COLS):
                columns[n][u] = step(columns[n][u], column, inverse, j)
    return [m[:, COLS:] for m in mats]


def kernel(
    cols_hbm, lost_hbm, tiles_ref, pre_hbm, b_hbm, rec_ref, tres_ref,
    stage, zstage, hl, zhl, win, winb, winc, rhs, msg0, msg1, msg2, near0, near1, near2, far0, far1, side, shot, shot_msg, cols_ref, lost_ref, local,
    load_sem, hs_sem, hr_sem, ns_sem, nr_sem, fs_sem, fr_sem, as_sem, ar_sem,
):
    g = lax.axis_index("grp")
    r = lax.axis_index("row")
    d = g * N_ROW + r
    cell = r // CELL
    pos = lax.rem(r, CELL)
    my_far = g * CELLS + cell
    first = d * BR - BAND
    total_devices = N_GRP * N_ROW

    def place(step_z, step_c):
        return lax.rem(pos // 2 + step_z, CELL // 2) * 2 + lax.rem(pos + step_c, 2)

    def near_dev(step):
        return (g, cell * CELL + place(*step))

    def far_dev(step):
        return (lax.rem(g + step[0], N_GRP), lax.rem(cell + step[1], CELLS) * CELL + pos)

    def shot_dev(step):
        return (g, lax.rem(cell + step[0], CELLS) * CELL + place(*step[1:]))

    def halo_dev(o):
        t = lax.rem(d + o + total_devices, total_devices)
        return (t // N_ROW, lax.rem(t, N_ROW))

    border = jnp.logical_or(r < REACH, r >= N_ROW - REACH)
    offsets = [3, -3, 2, -2, 1, -1]
    fars = [far0, far1]
    nears = [near0, near1, near2]
    msgs = [msg0, msg1, msg2]

    barrier = pltpu.get_barrier_semaphore()
    for o in offsets:
        pl.semaphore_signal(barrier, inc=1, device_id=halo_dev(o), device_id_type=MESH)
    for n in FAR_STEPS:
        pl.semaphore_signal(barrier, inc=1, device_id=far_dev(n), device_id_type=MESH)
    for n in NEAR_STEPS:
        pl.semaphore_signal(barrier, inc=1, device_id=near_dev(n), device_id_type=MESH)

    own_span = pl.ds(BAND, BR)
    loads = [
        pltpu.make_async_copy(b_hbm, win.at[WB, own_span], load_sem.at[0]),
        pltpu.make_async_copy(pre_hbm, zstage, load_sem.at[1]),
        pltpu.make_async_copy(cols_hbm, cols_ref, load_sem.at[2]),
        pltpu.make_async_copy(lost_hbm, lost_ref, load_sem.at[3]),
    ] + [pltpu.make_async_copy(tiles_ref.at[i], stage.at[i], load_sem.at[4 + i]) for i in range(BR)]
    for load in loads:
        load.start()

    def wait_bytes(ref, sem):
        pltpu.make_async_copy(ref, ref, sem).wait()

    def halo_send(w, start=0, count=BR):
        for o in offsets:
            pltpu.make_async_remote_copy(
                src_ref=win.at[w, pl.ds(BAND + start, count)],
                dst_ref=win.at[w, pl.ds((REACH - o) * BR + start, count)],
                send_sem=hs_sem.at[w],
                recv_sem=hr_sem.at[w],
                device_id=halo_dev(o),
                device_id_type=MESH,
            ).start()

    def halo_wait(w):
        wait_bytes(win.at[w, pl.ds(0, WIN - BR)], hr_sem.at[w])

    def near_send(gm, value):
        msg, near = msgs[gm], nears[gm]
        n_lanes = value.shape[1]
        value = jnp.concatenate([value, jnp.zeros((value.shape[0], TB - n_lanes), F32)], axis=1)
        msg[0] = value
        near[pos] = value
        for n in NEAR_STEPS:
            pltpu.make_async_remote_copy(
                src_ref=msg.at[0],
                dst_ref=near.at[pos],
                send_sem=ns_sem.at[gm],
                recv_sem=nr_sem.at[gm],
                device_id=near_dev(n),
                device_id_type=MESH,
            ).start()

    def near_sum(gm):
        msg, near = msgs[gm], nears[gm]
        wait_bytes(near.at[pl.ds(0, CELL - 1)], nr_sem.at[gm])
        terms = [near[n] for n in range(CELL)]
        while len(terms) > 1:
            terms = [terms[n] + terms[n + 1] for n in range(0, len(terms), 2)]
        msg[1] = terms[0]
        return terms[0]

    def far_send(gm):
        far = fars[gm]
        far[my_far] = near_sum(gm)
        for n in FAR_STEPS:
            pltpu.make_async_remote_copy(
                src_ref=msgs[gm].at[1],
                dst_ref=far.at[my_far],
                send_sem=fs_sem.at[gm],
                recv_sem=fr_sem.at[gm],
                device_id=far_dev(n),
                device_id_type=MESH,
            ).start()

    def far_all(gm):
        far = fars[gm]
        wait_bytes(far.at[pl.ds(0, FAR - 1)], fr_sem.at[gm])
        terms = [far[n] for n in range(FAR)]
        while len(terms) > 1:
            terms = [terms[n] + terms[n + 1] for n in range(0, len(terms), 2)]
        return terms[0]

    def side_send(gm):
        side[cell] = near_sum(gm)
        for n in (2, 1, 3):
            pltpu.make_async_remote_copy(
                src_ref=msgs[gm].at[1],
                dst_ref=side.at[cell],
                send_sem=fs_sem.at[gm],
                recv_sem=fr_sem.at[gm],
                device_id=(g, lax.rem(cell + n, CELLS) * CELL + pos),
                device_id_type=MESH,
            ).start()
        for step, target in ((1, 0), (N_GRP - 1, CELLS - 1)):
            pltpu.make_async_remote_copy(
                src_ref=msgs[gm].at[1],
                dst_ref=side.at[CELLS + cell],
                send_sem=as_sem.at[0],
                recv_sem=ar_sem.at[0],
                device_id=(lax.rem(g + step, N_GRP), target * CELL + pos),
                device_id_type=MESH,
            ).start()

    lost_of = [None]

    def side_sum(gm):
        wait_bytes(side.at[pl.ds(0, CELLS - 1)], fr_sem.at[gm])

        @pl.when(jnp.logical_or(cell == 0, cell == CELLS - 1))
        def _():
            wait_bytes(side.at[pl.ds(0, CELLS)], ar_sem.at[0])

        own = (side[0] + side[1]) + (side[2] + side[3])
        other = (side[4] + side[5]) + (side[6] + side[7])
        return jnp.where(lost_of[0], other, own)

    far_edges = [(1, 0), (1, 1), (1, 2), (N_GRP - 1, N_ROW - 1), (N_GRP - 1, N_ROW - 2), (N_GRP - 1, N_ROW - 3)]

    def folded(value):
        half = COLS // 2
        return jnp.concatenate([value[n * half : (n + 1) * half] for n in range(4)], axis=1)

    def unfolded(value):
        return jnp.concatenate([value[:, n * COLS : (n + 1) * COLS] for n in range(4)], axis=0)

    def shot_send(value):
        value = jnp.concatenate([folded(value), jnp.zeros((COLS // 2, TB - 4 * COLS), F32)], axis=1)
        shot_msg[...] = value
        shot[r] = value
        for step, target in far_edges:
            pltpu.make_async_remote_copy(
                src_ref=shot_msg,
                dst_ref=shot.at[N_ROW + r],
                send_sem=as_sem.at[1],
                recv_sem=ar_sem.at[1],
                device_id=(lax.rem(g + step, N_GRP), target),
                device_id_type=MESH,
            ).start()
        for n in SHOT_STEPS:
            pltpu.make_async_remote_copy(
                src_ref=shot_msg,
                dst_ref=shot.at[r],
                send_sem=fs_sem.at[3],
                recv_sem=fr_sem.at[3],
                device_id=shot_dev(n),
                device_id_type=MESH,
            ).start()

    def shot_sum():
        wait_bytes(shot.at[pl.ds(0, N_ROW - 1)], fr_sem.at[3])

        @pl.when(border)
        def _():
            wait_bytes(shot.at[pl.ds(0, N_ROW)], ar_sem.at[1])

        sums = []
        for at in (0, N_ROW):
            terms = [shot[at + n] for n in range(N_ROW)]
            while len(terms) > 1:
                terms = [terms[n] + terms[n + 1] for n in range(0, len(terms), 2)]
            sums.append(terms[0])
        return unfolded(jnp.where(lost_of[0], sums[1], sums[0]))

    def prepare(w, ref, at):
        for p in range(2 * REACH + 1):
            group = lax.rem(d + (p - REACH) + total_devices, total_devices) // N_ROW
            own = jnp.where(group == g, 1.0, 0.0).astype(BF16)
            for q in range(BR):
                hi, lo = split(win[w, p * BR + q])
                hi_own = hi * own
                lo_own = lo * own
                ref[p * BR + q, at : at + 4 * COLS] = jnp.concatenate(
                    [hi_own, lo_own, hi - hi_own, lo - lo_own], axis=0
                )

    def product(ref, count, after=None):
        own = [[] for _ in range(count)]
        other = [[] for _ in range(count)]
        rows = 4 * COLS * count
        for i in range(BR):
            for k in range(K):
                rhs[i, 0:rows, k * TB : (k + 1) * TB] = ref[local[i, k]]
            o = lax.dot_general(hl[i], rhs[i, 0:rows], (((1,), (1,)), ((), ())), preferred_element_type=F32)
            o = (o[:TB] + o[TB:]).T
            for n in range(count):
                own[n].append(o[4 * n * COLS : (4 * n + 1) * COLS] + o[(4 * n + 1) * COLS : (4 * n + 2) * COLS])
                other[n].append(
                    o[(4 * n + 2) * COLS : (4 * n + 3) * COLS] + o[(4 * n + 3) * COLS : (4 * n + 4) * COLS]
                )
            if after is not None:
                after(i, own[0][i], other[0][i])
        return [jnp.concatenate(v, axis=1) for v in own], [jnp.concatenate(v, axis=1) for v in other]

    def condition(*vectors):
        out = [[] for _ in vectors]
        for i in range(BR):
            parts = []
            for v in vectors:
                parts.extend(split(v[:, i * TB : (i + 1) * TB]))
            o = lax.dot_general(
                zhl[i], jnp.concatenate(parts, axis=0), (((1,), (1,)), ((), ())), preferred_element_type=F32
            )
            o = (o[:TB] + o[TB:]).T
            for n in range(len(vectors)):
                out[n].append(o[2 * n * COLS : (2 * n + 1) * COLS] + o[(2 * n + 1) * COLS : (2 * n + 2) * COLS])
        return [jnp.concatenate(v, axis=1) for v in out]

    def put(w, v):
        for i in range(BR):
            win[w, BAND + i] = v[:, i * TB : (i + 1) * TB]

    def lanes(m, *spans):
        return jnp.concatenate([m[a : a + COLS, b : b + n] for a, b, n in spans], axis=1)

    def stack(*parts):
        return jnp.concatenate(parts, axis=0)

    loads[0].wait()
    pl.semaphore_wait(barrier, len(offsets) + CELL - 1 + FAR - 1)
    halo_send(WB)
    loads[1].wait()
    for i in range(BR):
        hi, lo = split(zstage[i])
        zhl[i, 0:TB] = hi
        zhl[i, TB : 2 * TB] = lo
    v0 = jnp.concatenate([win[WB, BAND + i] for i in range(BR)], axis=1)
    (zb,) = condition(v0)
    put(WZ, zb)
    for n in range(CELLS):
        side[CELLS + n] = jnp.zeros((COLS, TB), F32)
    for n in range(N_ROW):
        shot[N_ROW + n] = jnp.zeros((COLS // 2, TB), F32)

    loads[2].wait()

    def localise(k, carry):
        for i in range(BR):
            local[i, k] = jnp.clip(cols_ref[i, k] - first, 0, WIN - 1)
        return carry

    lax.fori_loop(0, K, localise, 0)
    for i in range(BR):
        loads[4 + i].wait()

        def convert(k, carry, i=i):
            hi, lo = split(stage[i, k])
            at = pl.ds(pl.multiple_of(k * TB, TB), TB)
            hl[i, 0:TB, at] = hi
            hl[i, TB : 2 * TB, at] = lo
            return carry

        lax.fori_loop(0, K, convert, 0)
    halo_wait(WB)
    halo_send(WZ)
    prepare(WB, winb, 0)

    def send_rows(i, own, other):
        win[WV, BAND + i] = own + other - v0[:, i * TB : (i + 1) * TB]
        if i % 2 == 1:
            halo_send(WV, i - 1, 2)

    (own,), (p0,) = product(winb, 1, send_rows)
    v1 = own + p0 - v0
    (zp0,) = condition(p0)
    put(WP, zp0)
    basis = stack(v0, v1)
    ga = mm(basis, basis, 1, 1)
    near_send(0, lanes(ga, (0, 0, 32), (16, 0, 32)))
    loads[3].wait()
    lost = lax.rem(lost_ref[0], N_GRP)
    touch = jnp.logical_and(border, jnp.where(r < N_ROW // 2, g - 1, g + 1) == lost)
    is_lost = g == lost
    lost_of[0] = touch
    halo_wait(WZ)
    prepare(WZ, winc, 0)
    far_send(0)
    halo_wait(WV)
    halo_send(WP)
    prepare(WV, winb, 0)
    (own,), (p1,) = product(winb, 1)
    v2 = own + p1 - v1
    near_send(1, folded(mm(basis, v2, 1, 1)))
    (zp1,) = condition(p1)
    put(WQ, zp1)
    halo_send(WQ)
    one = eye16()
    ga = far_all(0)
    ga = stack(ga[:, 0:32], ga[:, 32:64])
    g00 = sym(ga[0:16, 0:16])
    half = sym(ga[0:16, 16:32])
    e0, inv0 = eliminate((g00 + half, half), (g00, one))
    a0 = one - e0
    c = stack(e0, -a0)
    squares = mm(c, mm(ga, c), 0, 0)
    far_send(1)
    m0 = mm(inv0, squares)
    d0 = e0 + m0
    d1 = -a0
    dd = stack(d0, d1)
    curve = mm(dd, mm(ga, stack(d0, d0 + d1)), 0, 0)
    halo_wait(WP)
    prepare(WP, winc, 4 * COLS)
    halo_wait(WQ)
    prepare(WQ, winc, 8 * COLS)
    (bz, bzp0, bzp1), (oz, ozp0, ozp1) = product(winc, 3)
    y, yp0, yp1 = condition(bz, bzp0, bzp1)
    gb = unfolded(far_all(1))
    curve = curve + mm(dd, mm(gb, d1), 0, 0)
    (a1,) = eliminate((sym(curve), squares))
    cs = mm(dd, a1) + stack(a0, jnp.zeros_like(a0))
    t0 = y - mm(cs, stack(yp0, yp1), 0, 0)
    put(WT, t0)
    halo_send(WT)
    coupled = mm(cs, stack(p0, p1), 0, 0)
    rr = v0 - coupled
    s0 = zb - mm(cs, stack(zp0, zp1), 0, 0)
    q0 = bz - mm(cs, stack(bzp0, bzp1), 0, 0)
    g2 = mm(stack(rr, s0, q0), stack(s0, q0, t0), 1, 1)
    near_send(2, lanes(g2, (0, 0, 16), (0, 32, 16), (16, 16, 16), (32, 32, 16)))
    ps0 = oz - mm(cs, stack(ozp0, ozp1), 0, 0)
    base_rec = mm(cs, basis, 0, 0)
    d0a = mm(d0, a1)
    d1a = mm(d1, a1)
    rc = stack(e0 - d0a, -(a0 + d0a + d1a), -d1a)
    residual = mm(rc, stack(v0, v1, v2), 0, 0)
    st = stack(s0, t0)
    side_send(2)
    halo_wait(WT)
    prepare(WT, winb, 0)
    (q1,), (ps1,) = product(winb, 1)
    g3 = mm(st, q1, 1, 1)
    shot_send(g3)
    g2 = side_sum(2)
    w0 = g2[:, 0:16]
    rt, sq, qt = g2[:, 16:32], g2[:, 32:48], g2[:, 48:64]
    b0, invw = eliminate((sym(sq), w0), (sym(w0), one))
    w1 = w0 - mm(rt, b0) + mm(b0, mm(qt, b0) - sq.T, 0, 0)
    n0 = one + mm(invw, w1)
    nb = stack(n0, -b0)
    bend = mm(nb, mm(stack(sq, qt.T), n0), 0, 0)
    base = jnp.where(is_lost, rr, residual + jnp.where(touch, coupled, 0.0))
    xs = stack(jnp.where(is_lost, q0, ps0), jnp.where(is_lost, q1, ps1))
    g3 = shot_sum()
    bend = bend - mm(nb, mm(g3, b0), 0, 0)
    (b1,) = eliminate((sym(bend), w1))
    es = mm(nb, b1) + stack(b0, jnp.zeros_like(b0))
    rec = jnp.where(is_lost, mm(es, st, 0, 0), base_rec)
    tres = jnp.where(jnp.logical_or(is_lost, touch), base - mm(es, xs, 0, 0), base)
    for i in range(BR):
        rec_ref[i] = rec[:, i * TB : (i + 1) * TB]
        tres_ref[i] = tres[:, i * TB : (i + 1) * TB]
    for w in range(WINS):
        wait_bytes(win.at[w, pl.ds(0, WIN - BR)], hs_sem.at[w])
    for gm in range(3):
        wait_bytes(nears[gm].at[pl.ds(0, CELL - 1)], ns_sem.at[gm])
    for gm in range(2):
        wait_bytes(fars[gm].at[pl.ds(0, FAR - 1)], fs_sem.at[gm])
    wait_bytes(side.at[pl.ds(0, CELLS - 1)], fs_sem.at[2])
    wait_bytes(side.at[pl.ds(0, 2)], as_sem.at[0])
    wait_bytes(shot.at[pl.ds(0, N_ROW - 1)], fs_sem.at[3])
    wait_bytes(shot.at[pl.ds(0, len(far_edges))], as_sem.at[1])


def per_device(matrix_tiles, column_index, precond, right_side, lost_group):
    vmem = pl.BlockSpec(memory_space=pltpu.VMEM)
    hbm = pl.BlockSpec(memory_space=pltpu.HBM)
    shape = jax.ShapeDtypeStruct((BR, COLS, TB), F32)
    dma = pltpu.SemaphoreType.DMA
    return pl.pallas_call(
        kernel,
        out_shape=(shape, shape),
        in_specs=[hbm, hbm, hbm, hbm, hbm],
        out_specs=(vmem, vmem),
        scratch_shapes=[
            pltpu.VMEM((BR, K, TB, TB), F32),
            pltpu.VMEM((BR, TB, TB), F32),
            pltpu.VMEM((BR, 2 * TB, K * TB), BF16),
            pltpu.VMEM((BR, 2 * TB, TB), BF16),
            pltpu.VMEM((WINS, WIN, COLS, TB), F32),
            pltpu.VMEM((WIN, 4 * COLS, TB), BF16),
            pltpu.VMEM((WIN, 12 * COLS, TB), BF16),
            pltpu.VMEM((BR, 12 * COLS, K * TB), BF16),
            pltpu.VMEM((2, COLS, TB), F32),
            pltpu.VMEM((2, COLS // 2, TB), F32),
            pltpu.VMEM((2, COLS, TB), F32),
            pltpu.VMEM((CELL, COLS, TB), F32),
            pltpu.VMEM((CELL, COLS // 2, TB), F32),
            pltpu.VMEM((CELL, COLS, TB), F32),
            pltpu.VMEM((FAR, COLS, TB), F32),
            pltpu.VMEM((FAR, COLS // 2, TB), F32),
            pltpu.VMEM((2 * CELLS, COLS, TB), F32),
            pltpu.VMEM((2 * N_ROW, COLS // 2, TB), F32),
            pltpu.VMEM((COLS // 2, TB), F32),
            pltpu.SMEM((BR, K), jnp.int32),
            pltpu.SMEM((1,), jnp.int32),
            pltpu.SMEM((BR, K), jnp.int32),
            dma((4 + BR,)),
            dma((WINS,)),
            dma((WINS,)),
            dma((3,)),
            dma((3,)),
            dma((4,)),
            dma((4,)),
            dma((2,)),
            dma((2,)),
        ],
        compiler_params=pltpu.CompilerParams(
            collective_id=0, has_side_effects=True, vmem_limit_bytes=55136 * 1024
        ),
        name="recover",
    )(column_index, lost_group, matrix_tiles, precond, right_side)


def solution(mesh):
    in_specs = (
        P(("grp", "row"), None, None, None),
        P(("grp", "row"), None),
        P(("grp", "row"), None, None),
        P(("grp", "row"), None, None),
        P(),
    )
    out_specs = (P(("grp", "row"), None, None), P(("grp", "row"), None, None))
    return jax.shard_map(
        per_device, mesh=mesh, in_specs=in_specs, out_specs=out_specs, check_vma=False
    )
```

```python
import functools

import jax
import jax.numpy as jnp
from jax import lax
from jax.experimental import pallas as pl
from jax.experimental.pallas import tpu as pltpu
from jax.sharding import PartitionSpec as P

BAND = 12
F32 = jnp.float32
BF16 = jnp.bfloat16
MESH = pl.DeviceIdType.MESH
N_GRP, N_ROW, BR, K, COLS, TB = 4, 32, 4, 32, 16, 128
REACH = 3
WIN = BR * (2 * REACH + 1)
CELL = 8
FAR = (N_GRP * N_ROW) // CELL
CELLS = N_ROW // CELL
WB, WZ, WV, WP, WQ, WT = range(6)
WINS = 6


def farthest_first(steps):
    def hops(step):
        return -sum(min(n, size - n) * weight for n, size, weight in zip(step, *steps[1:]))

    return sorted(steps[0], key=hops)


NEAR_STEPS = farthest_first(([(z, c) for z in range(4) for c in range(2) if z + c], (4, 2), (2, 1)))
FAR_STEPS = farthest_first(([(x, y) for x in range(4) for y in range(4) if x + y], (4, 4), (1, 1)))
SHOT_STEPS = farthest_first(
    ([(y, z, c) for y in range(4) for z in range(4) for c in range(2) if y + z + c], (4, 4, 2), (2, 2, 1))
)


def mm(a, b, ca=1, cb=0):
    return lax.dot_general(
        a, b, (((ca,), (cb,)), ((), ())), precision=lax.Precision.HIGHEST, preferred_element_type=F32
    )


def split(x):
    hi = x.astype(BF16)
    return hi, (x - hi.astype(F32)).astype(BF16)


def eye16():
    r = lax.broadcasted_iota(jnp.int32, (COLS, COLS), 0)
    c = lax.broadcasted_iota(jnp.int32, (COLS, COLS), 1)
    return (r == c).astype(F32)


def sym(g):
    return 0.5 * (g + g.T)


def eliminate(*systems):
    mats = [jnp.concatenate([s, h], axis=1) for s, h in systems]
    shape = mats[0].shape
    rows = lax.broadcasted_iota(jnp.int32, shape, 0)
    columns = [[jnp.broadcast_to(m[:, j : j + 1], shape) for j in range(COLS)] for m in mats]

    def step(value, column, inverse, j):
        row = value[j : j + 1] * inverse
        return jnp.where(rows == j, row, value - column * row)

    for j in range(COLS):
        for n in range(len(mats)):
            column = columns[n][j]
            inverse = 1.0 / column[j : j + 1]
            mats[n] = step(mats[n], column, inverse, j)
            for u in range(j + 1, COLS):
                columns[n][u] = step(columns[n][u], column, inverse, j)
    return [m[:, COLS:] for m in mats]


def kernel(
    cols_hbm, lost_hbm, tiles_ref, pre_hbm, b_hbm, rec_ref, tres_ref,
    stage, zstage, hl, zhl, win, winb, winc, rhs, msg0, msg1, msg2, near0, near1, near2, far0, far1, side, shot, shot_msg, cols_ref, lost_ref, local,
    load_sem, hs_sem, hr_sem, ns_sem, nr_sem, fs_sem, fr_sem, as_sem, ar_sem,
):
    g = lax.axis_index("grp")
    r = lax.axis_index("row")
    d = g * N_ROW + r
    cell = r // CELL
    pos = lax.rem(r, CELL)
    my_far = g * CELLS + cell
    first = d * BR - BAND
    total_devices = N_GRP * N_ROW

    def place(step_z, step_c):
        return lax.rem(pos // 2 + step_z, CELL // 2) * 2 + lax.rem(pos + step_c, 2)

    def near_dev(step):
        return (g, cell * CELL + place(*step))

    def far_dev(step):
        return (lax.rem(g + step[0], N_GRP), lax.rem(cell + step[1], CELLS) * CELL + pos)

    def shot_dev(step):
        return (g, lax.rem(cell + step[0], CELLS) * CELL + place(*step[1:]))

    def halo_dev(o):
        t = lax.rem(d + o + total_devices, total_devices)
        return (t // N_ROW, lax.rem(t, N_ROW))

    border = jnp.logical_or(r < REACH, r >= N_ROW - REACH)
    offsets = [3, -3, 2, -2, 1, -1]
    fars = [far0, far1]
    nears = [near0, near1, near2]
    msgs = [msg0, msg1, msg2]

    barrier = pltpu.get_barrier_semaphore()
    for o in offsets:
        pl.semaphore_signal(barrier, inc=1, device_id=halo_dev(o), device_id_type=MESH)
    for n in FAR_STEPS:
        pl.semaphore_signal(barrier, inc=1, device_id=far_dev(n), device_id_type=MESH)
    for n in NEAR_STEPS:
        pl.semaphore_signal(barrier, inc=1, device_id=near_dev(n), device_id_type=MESH)

    own_span = pl.ds(BAND, BR)
    loads = [
        pltpu.make_async_copy(b_hbm, win.at[WB, own_span], load_sem.at[0]),
        pltpu.make_async_copy(pre_hbm, zstage, load_sem.at[1]),
        pltpu.make_async_copy(cols_hbm, cols_ref, load_sem.at[2]),
        pltpu.make_async_copy(lost_hbm, lost_ref, load_sem.at[3]),
    ] + [pltpu.make_async_copy(tiles_ref.at[i], stage.at[i], load_sem.at[4 + i]) for i in range(BR)]
    for load in loads:
        load.start()

    def wait_bytes(ref, sem):
        pltpu.make_async_copy(ref, ref, sem).wait()

    def halo_send(w, start=0, count=BR):
        for o in offsets:
            pltpu.make_async_remote_copy(
                src_ref=win.at[w, pl.ds(BAND + start, count)],
                dst_ref=win.at[w, pl.ds((REACH - o) * BR + start, count)],
                send_sem=hs_sem.at[w],
                recv_sem=hr_sem.at[w],
                device_id=halo_dev(o),
                device_id_type=MESH,
            ).start()

    def halo_wait(w):
        wait_bytes(win.at[w, pl.ds(0, WIN - BR)], hr_sem.at[w])

    def near_send(gm, value):
        msg, near = msgs[gm], nears[gm]
        n_lanes = value.shape[1]
        value = jnp.concatenate([value, jnp.zeros((value.shape[0], TB - n_lanes), F32)], axis=1)
        msg[0] = value
        near[pos] = value
        for n in NEAR_STEPS:
            pltpu.make_async_remote_copy(
                src_ref=msg.at[0],
                dst_ref=near.at[pos],
                send_sem=ns_sem.at[gm],
                recv_sem=nr_sem.at[gm],
                device_id=near_dev(n),
                device_id_type=MESH,
            ).start()

    def near_sum(gm):
        msg, near = msgs[gm], nears[gm]
        wait_bytes(near.at[pl.ds(0, CELL - 1)], nr_sem.at[gm])
        terms = [near[n] for n in range(CELL)]
        while len(terms) > 1:
            terms = [terms[n] + terms[n + 1] for n in range(0, len(terms), 2)]
        msg[1] = terms[0]
        return terms[0]

    def far_send(gm):
        far = fars[gm]
        far[my_far] = near_sum(gm)
        for n in FAR_STEPS:
            pltpu.make_async_remote_copy(
                src_ref=msgs[gm].at[1],
                dst_ref=far.at[my_far],
                send_sem=fs_sem.at[gm],
                recv_sem=fr_sem.at[gm],
                device_id=far_dev(n),
                device_id_type=MESH,
            ).start()

    def far_all(gm):
        far = fars[gm]
        wait_bytes(far.at[pl.ds(0, FAR - 1)], fr_sem.at[gm])
        terms = [far[n] for n in range(FAR)]
        while len(terms) > 1:
            terms = [terms[n] + terms[n + 1] for n in range(0, len(terms), 2)]
        return terms[0]

    def side_send(gm):
        side[cell] = near_sum(gm)
        for n in (2, 1, 3):
            pltpu.make_async_remote_copy(
                src_ref=msgs[gm].at[1],
                dst_ref=side.at[cell],
                send_sem=fs_sem.at[gm],
                recv_sem=fr_sem.at[gm],
                device_id=(g, lax.rem(cell + n, CELLS) * CELL + pos),
                device_id_type=MESH,
            ).start()
        for step, target in ((1, 0), (N_GRP - 1, CELLS - 1)):
            pltpu.make_async_remote_copy(
                src_ref=msgs[gm].at[1],
                dst_ref=side.at[CELLS + cell],
                send_sem=as_sem.at[0],
                recv_sem=ar_sem.at[0],
                device_id=(lax.rem(g + step, N_GRP), target * CELL + pos),
                device_id_type=MESH,
            ).start()

    lost_of = [None]

    def side_sum(gm):
        wait_bytes(side.at[pl.ds(0, CELLS - 1)], fr_sem.at[gm])

        @pl.when(jnp.logical_or(cell == 0, cell == CELLS - 1))
        def _():
            wait_bytes(side.at[pl.ds(0, CELLS)], ar_sem.at[0])

        own = (side[0] + side[1]) + (side[2] + side[3])
        other = (side[4] + side[5]) + (side[6] + side[7])
        return jnp.where(lost_of[0], other, own)

    far_edges = [(1, 0), (1, 1), (1, 2), (N_GRP - 1, N_ROW - 1), (N_GRP - 1, N_ROW - 2), (N_GRP - 1, N_ROW - 3)]

    def folded(value):
        half = COLS // 2
        return jnp.concatenate([value[n * half : (n + 1) * half] for n in range(4)], axis=1)

    def unfolded(value):
        return jnp.concatenate([value[:, n * COLS : (n + 1) * COLS] for n in range(4)], axis=0)

    def shot_send(value):
        value = jnp.concatenate([folded(value), jnp.zeros((COLS // 2, TB - 4 * COLS), F32)], axis=1)
        shot_msg[...] = value
        shot[r] = value
        for step, target in far_edges:
            pltpu.make_async_remote_copy(
                src_ref=shot_msg,
                dst_ref=shot.at[N_ROW + r],
                send_sem=as_sem.at[1],
                recv_sem=ar_sem.at[1],
                device_id=(lax.rem(g + step, N_GRP), target),
                device_id_type=MESH,
            ).start()
        for n in SHOT_STEPS:
            pltpu.make_async_remote_copy(
                src_ref=shot_msg,
                dst_ref=shot.at[r],
                send_sem=fs_sem.at[3],
                recv_sem=fr_sem.at[3],
                device_id=shot_dev(n),
                device_id_type=MESH,
            ).start()

    def shot_sum():
        wait_bytes(shot.at[pl.ds(0, N_ROW - 1)], fr_sem.at[3])

        @pl.when(border)
        def _():
            wait_bytes(shot.at[pl.ds(0, N_ROW)], ar_sem.at[1])

        sums = []
        for at in (0, N_ROW):
            terms = [shot[at + n] for n in range(N_ROW)]
            while len(terms) > 1:
                terms = [terms[n] + terms[n + 1] for n in range(0, len(terms), 2)]
            sums.append(terms[0])
        return unfolded(jnp.where(lost_of[0], sums[1], sums[0]))

    def prepare(w, ref, at):
        for p in range(2 * REACH + 1):
            group = lax.rem(d + (p - REACH) + total_devices, total_devices) // N_ROW
            own = jnp.where(group == g, 1.0, 0.0).astype(BF16)
            for q in range(BR):
                hi, lo = split(win[w, p * BR + q])
                hi_own = hi * own
                lo_own = lo * own
                ref[p * BR + q, at : at + 4 * COLS] = jnp.concatenate(
                    [hi_own, lo_own, hi - hi_own, lo - lo_own], axis=0
                )

    def product(ref, count, after=None):
        own = [[] for _ in range(count)]
        other = [[] for _ in range(count)]
        rows = 4 * COLS * count
        for i in range(BR):
            for k in range(K):
                rhs[i, 0:rows, k * TB : (k + 1) * TB] = ref[local[i, k]]
            o = lax.dot_general(hl[i], rhs[i, 0:rows], (((1,), (1,)), ((), ())), preferred_element_type=F32)
            o = (o[:TB] + o[TB:]).T
            for n in range(count):
                own[n].append(o[4 * n * COLS : (4 * n + 1) * COLS] + o[(4 * n + 1) * COLS : (4 * n + 2) * COLS])
                other[n].append(
                    o[(4 * n + 2) * COLS : (4 * n + 3) * COLS] + o[(4 * n + 3) * COLS : (4 * n + 4) * COLS]
                )
            if after is not None:
                after(i, own[0][i], other[0][i])
        return [jnp.concatenate(v, axis=1) for v in own], [jnp.concatenate(v, axis=1) for v in other]

    def condition(*vectors):
        out = [[] for _ in vectors]
        for i in range(BR):
            parts = []
            for v in vectors:
                parts.extend(split(v[:, i * TB : (i + 1) * TB]))
            o = lax.dot_general(
                zhl[i], jnp.concatenate(parts, axis=0), (((1,), (1,)), ((), ())), preferred_element_type=F32
            )
            o = (o[:TB] + o[TB:]).T
            for n in range(len(vectors)):
                out[n].append(o[2 * n * COLS : (2 * n + 1) * COLS] + o[(2 * n + 1) * COLS : (2 * n + 2) * COLS])
        return [jnp.concatenate(v, axis=1) for v in out]

    def put(w, v):
        for i in range(BR):
            win[w, BAND + i] = v[:, i * TB : (i + 1) * TB]

    def lanes(m, *spans):
        return jnp.concatenate([m[a : a + COLS, b : b + n] for a, b, n in spans], axis=1)

    def stack(*parts):
        return jnp.concatenate(parts, axis=0)

    loads[0].wait()
    pl.semaphore_wait(barrier, len(offsets) + CELL - 1 + FAR - 1)
    halo_send(WB)
    loads[1].wait()
    for i in range(BR):
        hi, lo = split(zstage[i])
        zhl[i, 0:TB] = hi
        zhl[i, TB : 2 * TB] = lo
    v0 = jnp.concatenate([win[WB, BAND + i] for i in range(BR)], axis=1)
    (zb,) = condition(v0)
    put(WZ, zb)
    for n in range(CELLS):
        side[CELLS + n] = jnp.zeros((COLS, TB), F32)
    for n in range(N_ROW):
        shot[N_ROW + n] = jnp.zeros((COLS // 2, TB), F32)

    loads[2].wait()

    def localise(k, carry):
        for i in range(BR):
            local[i, k] = jnp.clip(cols_ref[i, k] - first, 0, WIN - 1)
        return carry

    lax.fori_loop(0, K, localise, 0)
    for i in range(BR):
        loads[4 + i].wait()

        def convert(k, carry, i=i):
            hi, lo = split(stage[i, k])
            at = pl.ds(pl.multiple_of(k * TB, TB), TB)
            hl[i, 0:TB, at] = hi
            hl[i, TB : 2 * TB, at] = lo
            return carry

        lax.fori_loop(0, K, convert, 0)
    halo_wait(WB)
    halo_send(WZ)
    prepare(WB, winb, 0)

    def send_rows(i, own, other):
        win[WV, BAND + i] = own + other - v0[:, i * TB : (i + 1) * TB]
        halo_send(WV, i, 1)

    (own,), (p0,) = product(winb, 1, send_rows)
    v1 = own + p0 - v0
    (zp0,) = condition(p0)
    put(WP, zp0)
    basis = stack(v0, v1)
    ga = mm(basis, basis, 1, 1)
    near_send(0, lanes(ga, (0, 0, 32), (16, 0, 32)))
    loads[3].wait()
    lost = lax.rem(lost_ref[0], N_GRP)
    touch = jnp.logical_and(border, jnp.where(r < N_ROW // 2, g - 1, g + 1) == lost)
    is_lost = g == lost
    lost_of[0] = touch
    halo_wait(WZ)
    prepare(WZ, winc, 0)
    far_send(0)
    halo_wait(WV)
    halo_send(WP)
    prepare(WV, winb, 0)
    (own,), (p1,) = product(winb, 1)
    v2 = own + p1 - v1
    near_send(1, folded(mm(basis, v2, 1, 1)))
    (zp1,) = condition(p1)
    put(WQ, zp1)
    halo_send(WQ)
    one = eye16()
    ga = far_all(0)
    ga = stack(ga[:, 0:32], ga[:, 32:64])
    g00 = sym(ga[0:16, 0:16])
    half = sym(ga[0:16, 16:32])
    e0, inv0 = eliminate((g00 + half, half), (g00, one))
    a0 = one - e0
    c = stack(e0, -a0)
    squares = mm(c, mm(ga, c), 0, 0)
    far_send(1)
    m0 = mm(inv0, squares)
    d0 = e0 + m0
    d1 = -a0
    dd = stack(d0, d1)
    curve = mm(dd, mm(ga, stack(d0, d0 + d1)), 0, 0)
    halo_wait(WP)
    prepare(WP, winc, 4 * COLS)
    halo_wait(WQ)
    prepare(WQ, winc, 8 * COLS)
    (bz, bzp0, bzp1), (oz, ozp0, ozp1) = product(winc, 3)
    y, yp0, yp1 = condition(bz, bzp0, bzp1)
    gb = unfolded(far_all(1))
    curve = curve + mm(dd, mm(gb, d1), 0, 0)
    (a1,) = eliminate((sym(curve), squares))
    cs = mm(dd, a1) + stack(a0, jnp.zeros_like(a0))
    t0 = y - mm(cs, stack(yp0, yp1), 0, 0)
    put(WT, t0)
    halo_send(WT)
    coupled = mm(cs, stack(p0, p1), 0, 0)
    rr = v0 - coupled
    s0 = zb - mm(cs, stack(zp0, zp1), 0, 0)
    q0 = bz - mm(cs, stack(bzp0, bzp1), 0, 0)
    g2 = mm(stack(rr, s0, q0), stack(s0, q0, t0), 1, 1)
    near_send(2, lanes(g2, (0, 0, 16), (0, 32, 16), (16, 16, 16), (32, 32, 16)))
    ps0 = oz - mm(cs, stack(ozp0, ozp1), 0, 0)
    base_rec = mm(cs, basis, 0, 0)
    d0a = mm(d0, a1)
    d1a = mm(d1, a1)
    rc = stack(e0 - d0a, -(a0 + d0a + d1a), -d1a)
    residual = mm(rc, stack(v0, v1, v2), 0, 0)
    st = stack(s0, t0)
    side_send(2)
    halo_wait(WT)
    prepare(WT, winb, 0)
    (q1,), (ps1,) = product(winb, 1)
    g3 = mm(st, q1, 1, 1)
    shot_send(g3)
    g2 = side_sum(2)
    w0 = g2[:, 0:16]
    rt, sq, qt = g2[:, 16:32], g2[:, 32:48], g2[:, 48:64]
    b0, invw = eliminate((sym(sq), w0), (sym(w0), one))
    w1 = w0 - mm(rt, b0) + mm(b0, mm(qt, b0) - sq.T, 0, 0)
    n0 = one + mm(invw, w1)
    nb = stack(n0, -b0)
    bend = mm(nb, mm(stack(sq, qt.T), n0), 0, 0)
    base = jnp.where(is_lost, rr, residual + jnp.where(touch, coupled, 0.0))
    xs = stack(jnp.where(is_lost, q0, ps0), jnp.where(is_lost, q1, ps1))
    g3 = shot_sum()
    bend = bend - mm(nb, mm(g3, b0), 0, 0)
    (b1,) = eliminate((sym(bend), w1))
    es = mm(nb, b1) + stack(b0, jnp.zeros_like(b0))
    rec = jnp.where(is_lost, mm(es, st, 0, 0), base_rec)
    tres = jnp.where(jnp.logical_or(is_lost, touch), base - mm(es, xs, 0, 0), base)
    for i in range(BR):
        rec_ref[i] = rec[:, i * TB : (i + 1) * TB]
        tres_ref[i] = tres[:, i * TB : (i + 1) * TB]
    for w in range(WINS):
        wait_bytes(win.at[w, pl.ds(0, WIN - BR)], hs_sem.at[w])
    for gm in range(3):
        wait_bytes(nears[gm].at[pl.ds(0, CELL - 1)], ns_sem.at[gm])
    for gm in range(2):
        wait_bytes(fars[gm].at[pl.ds(0, FAR - 1)], fs_sem.at[gm])
    wait_bytes(side.at[pl.ds(0, CELLS - 1)], fs_sem.at[2])
    wait_bytes(side.at[pl.ds(0, 2)], as_sem.at[0])
    wait_bytes(shot.at[pl.ds(0, N_ROW - 1)], fs_sem.at[3])
    wait_bytes(shot.at[pl.ds(0, len(far_edges))], as_sem.at[1])


def per_device(matrix_tiles, column_index, precond, right_side, lost_group):
    vmem = pl.BlockSpec(memory_space=pltpu.VMEM)
    hbm = pl.BlockSpec(memory_space=pltpu.HBM)
    shape = jax.ShapeDtypeStruct((BR, COLS, TB), F32)
    dma = pltpu.SemaphoreType.DMA
    return pl.pallas_call(
        kernel,
        out_shape=(shape, shape),
        in_specs=[hbm, hbm, hbm, hbm, hbm],
        out_specs=(vmem, vmem),
        scratch_shapes=[
            pltpu.VMEM((BR, K, TB, TB), F32),
            pltpu.VMEM((BR, TB, TB), F32),
            pltpu.VMEM((BR, 2 * TB, K * TB), BF16),
            pltpu.VMEM((BR, 2 * TB, TB), BF16),
            pltpu.VMEM((WINS, WIN, COLS, TB), F32),
            pltpu.VMEM((WIN, 4 * COLS, TB), BF16),
            pltpu.VMEM((WIN, 12 * COLS, TB), BF16),
            pltpu.VMEM((BR, 12 * COLS, K * TB), BF16),
            pltpu.VMEM((2, COLS, TB), F32),
            pltpu.VMEM((2, COLS // 2, TB), F32),
            pltpu.VMEM((2, COLS, TB), F32),
            pltpu.VMEM((CELL, COLS, TB), F32),
            pltpu.VMEM((CELL, COLS // 2, TB), F32),
            pltpu.VMEM((CELL, COLS, TB), F32),
            pltpu.VMEM((FAR, COLS, TB), F32),
            pltpu.VMEM((FAR, COLS // 2, TB), F32),
            pltpu.VMEM((2 * CELLS, COLS, TB), F32),
            pltpu.VMEM((2 * N_ROW, COLS // 2, TB), F32),
            pltpu.VMEM((COLS // 2, TB), F32),
            pltpu.SMEM((BR, K), jnp.int32),
            pltpu.SMEM((1,), jnp.int32),
            pltpu.SMEM((BR, K), jnp.int32),
            dma((4 + BR,)),
            dma((WINS,)),
            dma((WINS,)),
            dma((3,)),
            dma((3,)),
            dma((4,)),
            dma((4,)),
            dma((2,)),
            dma((2,)),
        ],
        compiler_params=pltpu.CompilerParams(
            collective_id=0, has_side_effects=True, vmem_limit_bytes=55136 * 1024
        ),
        name="recover",
    )(column_index, lost_group, matrix_tiles, precond, right_side)


def solution(mesh):
    in_specs = (
        P(("grp", "row"), None, None, None),
        P(("grp", "row"), None),
        P(("grp", "row"), None, None),
        P(("grp", "row"), None, None),
        P(),
    )
    out_specs = (P(("grp", "row"), None, None), P(("grp", "row"), None, None))
    return jax.shard_map(
        per_device, mesh=mesh, in_specs=in_specs, out_specs=out_specs, check_vma=False
    )
```
